32 devices in a mesh: dom: 4 (over x, core), sub: 8 (over z, y).
Axes of the slice: x: 2, y: 2, z: 4, core: 2. Of those that a mesh axis runs over, the one named last changes fastest.
Arguments:
- node_feat: bfloat16 [96, 192, 128], P('dom', 'sub'), may hold values from -6 to 6
- edge_feat: bfloat16 [32768, 128], P(('dom', 'sub')), may hold values from -6 to 6
- edge_dst: int32 [32768], P(('dom', 'sub')), may hold values from 0 to 575
- edge_dir: int32 [32768], P(('dom', 'sub')), may hold values from 0 to 3, as said below
- edge_count: int32 [32], P(('dom', 'sub')), may hold values from 512 to 1024, as said below
- w_edge_in: bfloat16 [384, 128], P('dom'), may hold values from -0.3125 to 0.3125
- w_edge_out: bfloat16 [128, 128], P('dom'), may hold values from -0.5 to 0.5
- w_node_in: bfloat16 [256, 128], P('dom'), may hold values from -0.375 to 0.375
- w_node_out: bfloat16 [128, 128], P('dom'), may hold values from -0.5 to 0.5
- gains: bfloat16 [2, 128], P(None, 'dom'), may hold values from 0.099609375 to 1.8984375
- node_cot: bfloat16 [96, 192, 128], P('dom', 'sub'), may hold values from -6 to 6
- edge_cot: bfloat16 [32768, 128], P(('dom', 'sub')), may hold values from -6 to 6
Outputs:
- node_grad: bfloat16 [96, 192, 128], P('dom', 'sub')
- edge_grad: bfloat16 [32768, 128], P(('dom', 'sub'))
- w_edge_in_grad: float32 [384, 128], P('dom')
- w_edge_out_grad: float32 [128, 128], P('dom')
- w_node_in_grad: float32 [256, 128], P('dom')
- w_node_out_grad: float32 [128, 128], P('dom')
- gain_grad: float32 [2, 128], P(None, 'dom')
The draws below stay inside these ranges and needn't reach their ends.
Inputs may be any that keep to these rules, and one draw needn't show every extreme that they name: `edge_dir`: the sender lies inside the global grid. A device's live edges are its first edge_count slots; some device is full.
All inputs are finite; a program needn't handle non-finite values.
Results may differ from the reference program's by a relative error of at most 0.033.
The reference program's roundings to bfloat16 on the way count: a program that leaves them out, or rounds other values in their place, can miss the bound.
Values may be sent and summed in bfloat16 or wider, within the bound.
A program may use at most 64 MiB of HBM per device.

```python
import jax
import jax.numpy as jnp
from jax import lax

F = 128
SIDE = 24
E_DEV = 1024
NX = 96
NY = 192
NODES = 18432
EDGES = 32768
N_DOM = 4
N_SUB = 8


def edge_layout(key):
    base = jax.random.fold_in(key, 7)
    key_dst, key_dir = jax.random.split(base)
    target_local = jax.random.randint(key_dst, (EDGES,), 0, SIDE * SIDE, dtype=jnp.int32)
    drawn = jax.random.randint(key_dir, (EDGES,), 0, 4, dtype=jnp.int32)
    device = jnp.arange(EDGES, dtype=jnp.int32) // E_DEV
    columns_dev = NY // SIDE
    grid_row = device // columns_dev * SIDE + target_local // SIDE
    grid_col = device % columns_dev * SIDE + target_local % SIDE
    outside = (drawn == 0) & (grid_row == NX - 1) | (drawn == 1) & (grid_row == 0) | (drawn == 2) & (grid_col == NY - 1) | (drawn == 3) & (grid_col == 0)
    flipped = drawn + 1 - 2 * (drawn % 2)
    return (target_local, jnp.where(outside, flipped, drawn).astype(jnp.int32))


def draw_edge_dst(key, part):
    return edge_layout(key)[0]


def draw_edge_dir(key, part):
    return edge_layout(key)[1]


def draw_edge_count(key, part):
    devices = EDGES // E_DEV
    counts = jax.random.randint(jax.random.fold_in(key, 11), (devices,), E_DEV // 2, E_DEV + 1, dtype=jnp.int32)
    return counts.at[0].set(E_DEV)


def block_levels(own_key, dims, shards, low, largest):
    gain = 1.0
    for position, shards_of in shards:
        draws = jax.random.uniform(jax.random.fold_in(jax.random.fold_in(own_key, 6), position), (shards_of,), jnp.float32, low / len(shards), largest / len(shards))
        gain = gain * jnp.repeat(jnp.exp(draws), dims[position] // shards_of).reshape((-1,) + (1,) * (len(dims) - 1 - position))
    return gain


def centred(rng, extent, deviation, bound, shards=(), held_as=jnp.bfloat16):
    values = deviation * jax.random.normal(rng, extent, jnp.float32)
    if shards:
        values = values * block_levels(rng, extent, shards, -0.22, 0.18)
    return jnp.clip(values, -bound, bound).astype(held_as)


def setup_inputs(seed: int = 0) -> dict:
    key_of = jax.random.split(jax.random.key(seed), 13)
    node_feat = centred(key_of[0], (NX, NY, F), 1.0, 6.0, ((0, 4), (1, 8)))
    edge_feat = centred(key_of[1], (EDGES, F), 1.0, 6.0, ((0, 32),))
    edge_dst = draw_edge_dst(jax.random.fold_in(key_of[12], 71), 0)
    edge_dir = draw_edge_dir(jax.random.fold_in(key_of[12], 71), 0)
    edge_count = draw_edge_count(jax.random.fold_in(key_of[12], 71), 0)
    w_edge_in = centred(key_of[5], (3 * F, F), (3 * F) ** -0.5, 0.3125, ((0, 4),))
    w_edge_out = centred(key_of[6], (F, F), F ** -0.5, 0.5, ((0, 4),))
    w_node_in = centred(key_of[7], (2 * F, F), (2 * F) ** -0.5, 0.375, ((0, 4),))
    w_node_out = centred(key_of[8], (F, F), F ** -0.5, 0.5, ((0, 4),))
    gains = jnp.clip(1.0 + 0.18 * jax.random.normal(key_of[9], (2, F), jnp.float32), 0.099609375, 1.8984375).astype(jnp.bfloat16)
    node_cot = centred(key_of[10], (NX, NY, F), 1.0, 6.0, ((0, 4), (1, 8)))
    edge_cot = centred(key_of[11], (EDGES, F), 1.0, 6.0, ((0, 32),))
    return {"node_feat": node_feat, "edge_feat": edge_feat, "edge_dst": edge_dst, "edge_dir": edge_dir, "edge_count": edge_count, "w_edge_in": w_edge_in, "w_edge_out": w_edge_out, "w_node_in": w_node_in, "w_node_out": w_node_out, "gains": gains, "node_cot": node_cot, "edge_cot": edge_cot}


def layer_norm(raw_out):
    average = lax.optimization_barrier(jnp.mean(raw_out, axis=-1, keepdims=True))
    centered = raw_out - average
    inv_std = lax.rsqrt(lax.optimization_barrier(jnp.mean(centered * centered, axis=-1, keepdims=True)) + 1e-05)
    return (centered * inv_std, inv_std)

def norm_back(upstream, normed, inv_std):
    return (upstream - lax.optimization_barrier(jnp.mean(upstream, axis=-1, keepdims=True)) - normed * lax.optimization_barrier(jnp.mean(upstream * normed, axis=-1, keepdims=True))) * inv_std

def mlp_forward(inputs, w_first, w_second, gain_vec):
    pre_act = jnp.dot(inputs, w_first, preferred_element_type=jnp.float32)
    hidden = jnp.maximum(pre_act, 0.0).astype(jnp.bfloat16)
    raw_out = jnp.dot(hidden, w_second, preferred_element_type=jnp.float32)
    normed, inv_std = layer_norm(raw_out)
    return (pre_act, hidden, normed, inv_std, normed * gain_vec)

def mlp_backward(upstream, inputs, pre_act, hidden, normed, inv_std, gain_vec, w_first, w_second):
    gain_part = lax.optimization_barrier(jnp.sum(upstream * normed, axis=0))
    grad_raw = norm_back(upstream * gain_vec, normed, inv_std).astype(jnp.bfloat16)
    second_part = jnp.dot(hidden.T, grad_raw, preferred_element_type=jnp.float32)
    grad_hidden = jnp.dot(grad_raw, w_second.T, preferred_element_type=jnp.float32)
    grad_pre = jnp.where(pre_act > 0, grad_hidden, 0.0).astype(jnp.bfloat16)
    first_part = jnp.dot(inputs.T, grad_pre, preferred_element_type=jnp.float32)
    grad_inputs = jnp.dot(grad_pre, w_first.T, preferred_element_type=jnp.float32)
    return (grad_inputs, first_part, second_part, gain_part)

def reference(node_feat, edge_feat, edge_dst, edge_dir, edge_count, w_edge_in, w_edge_out, w_node_in, w_node_out, gains, node_cot, edge_cot):
    devices = N_DOM * N_SUB
    node_rows = node_feat.reshape(NODES, F)
    gain_edge = gains[0].astype(jnp.float32)
    gain_node = gains[1].astype(jnp.float32)
    feat_blocks = edge_feat.reshape(devices, E_DEV, F)
    cot_blocks = edge_cot.reshape(devices, E_DEV, F)
    dst_blocks = edge_dst.reshape(devices, E_DEV)
    dir_blocks = edge_dir.reshape(devices, E_DEV)
    device_ids = jnp.arange(devices, dtype=jnp.int32)

    def locate(target_local, direction, device):
        grid_row = device // N_SUB * SIDE + target_local // SIDE
        grid_col = device % N_SUB * SIDE + target_local % SIDE
        step_row = jnp.where(direction == 0, 1, jnp.where(direction == 1, -1, 0)).astype(jnp.int32)
        step_col = jnp.where(direction == 2, 1, jnp.where(direction == 3, -1, 0)).astype(jnp.int32)
        active = (jnp.arange(E_DEV, dtype=jnp.int32) < edge_count[device]).astype(jnp.float32)[:, None]
        target = (grid_row * NY + grid_col).astype(jnp.int32)
        source = ((grid_row + step_row) * NY + grid_col + step_col).astype(jnp.int32)
        return (target, source, active)

    def aggregate_pass(totals, blocks):
        features, target_local, direction, device = blocks
        target, source, active = locate(target_local, direction, device)
        inputs = jnp.concatenate([features, node_rows[source], node_rows[target]], axis=1)
        message = mlp_forward(inputs, w_edge_in, w_edge_out, gain_edge)[4]
        return (totals.at[target].add(message * active), None)
    aggregate, _ = lax.scan(aggregate_pass, jnp.zeros((NODES, F), jnp.float32), (feat_blocks, dst_blocks, dir_blocks, device_ids))
    node_input = jnp.concatenate([node_rows, aggregate.astype(jnp.bfloat16)], axis=1)
    pre_act, hidden, normed, inv_std, _ = mlp_forward(node_input, w_node_in, w_node_out, gain_node)
    node_upstream = node_cot.reshape(NODES, F).astype(jnp.float32)
    node_in_grad, node_first, node_second, node_gain = mlp_backward(node_upstream, node_input, pre_act, hidden, normed, inv_std, gain_node, w_node_in, w_node_out)
    agg_grad = node_in_grad[:, F:]

    def second(totals, blocks):
        spread_grad, first_sum, second_sum, gain_sum = totals
        features, cotangent, target_local, direction, device = blocks
        target, source, active = locate(target_local, direction, device)
        inputs = jnp.concatenate([features, node_rows[source], node_rows[target]], axis=1)
        pre_e, hidden_e, normed_e, inv_e, _ = mlp_forward(inputs, w_edge_in, w_edge_out, gain_edge)
        cot_float = cotangent.astype(jnp.float32)
        upstream = active * (cot_float + agg_grad[target])
        edge_in_grad, first_part, second_part, gain_part = mlp_backward(upstream, inputs, pre_e, hidden_e, normed_e, inv_e, gain_edge, w_edge_in, w_edge_out)
        edge_out = (cot_float + edge_in_grad[:, :F]).astype(jnp.bfloat16)
        spread_grad = spread_grad.at[source].add(edge_in_grad[:, F:2 * F]).at[target].add(edge_in_grad[:, 2 * F:])
        return ((spread_grad, first_sum + first_part, second_sum + second_part, gain_sum + gain_part), edge_out)
    start = (jnp.zeros((NODES, F), jnp.float32), jnp.zeros((3 * F, F), jnp.float32), jnp.zeros((F, F), jnp.float32), jnp.zeros((F,), jnp.float32))
    totals, edge_out = lax.scan(second, start, (feat_blocks, cot_blocks, dst_blocks, dir_blocks, device_ids))
    spread_grad, edge_first, edge_second, edge_gain = totals
    node_grad = (node_upstream + node_in_grad[:, :F] + spread_grad).astype(jnp.bfloat16).reshape(NX, NY, F)
    grad_scale = lax.rsqrt(jnp.float32(NODES))
    gain_grad = jnp.stack([edge_gain, node_gain]) * grad_scale
    return (node_grad, edge_out.reshape(EDGES, F), edge_first * grad_scale, edge_second * grad_scale, node_first * grad_scale, node_second * grad_scale, gain_grad)
```

```python
import functools

import jax
import jax.numpy as jnp
from jax import lax
from jax.experimental import pallas as pl
from jax.experimental.pallas import tpu as pltpu
from jax.sharding import PartitionSpec as P

MESH = pl.DeviceIdType.MESH
BF = jnp.bfloat16
F32 = jnp.float32
LANES = 128


def ceil_to(value, step):
    return -(-value // step) * step


def mm(a, b):
    return jnp.dot(a, b, preferred_element_type=F32)


def mm_nt(a, b):
    return lax.dot_general(a, b, (((1,), (1,)), ((), ())), preferred_element_type=F32)


def mm_tn(a, b):
    return lax.dot_general(a, b, (((0,), (0,)), ((), ())), preferred_element_type=F32)


def iota(shape, dim):
    return lax.broadcasted_iota(jnp.int32, shape, dim)


def one_hot(mask):
    return jnp.where(mask, 1.0, 0.0).astype(BF)


def layer_norm(raw_out):
    average = jnp.mean(raw_out, axis=-1, keepdims=True)
    centered = raw_out - average
    inv_std = lax.rsqrt(jnp.mean(centered * centered, axis=-1, keepdims=True) + 1e-05)
    return centered * inv_std, inv_std


def norm_back(upstream, normed, inv_std):
    return (
        upstream
        - jnp.mean(upstream, axis=-1, keepdims=True)
        - normed * jnp.mean(upstream * normed, axis=-1, keepdims=True)
    ) * inv_std


def split_rows(total, step):
    return [(at, min(step, total - at)) for at in range(0, total, step)]


class Plan:
    def __init__(self, n_dom, n_sub, side, edges, latent, rows):
        self.n_dom, self.n_sub = n_dom, n_sub
        self.side, self.edges, self.latent = side, edges, latent
        self.nodes = side * side
        self.own = ceil_to(self.nodes, LANES)
        self.strip = ceil_to(side, 16)
        self.halo = ceil_to(4 * self.strip, LANES)
        self.rows = rows
        at = 0
        self.off = {}
        for name in ("node_in", "node_out", "edge_in", "edge_out", "gains"):
            self.off[name] = at
            at += 16 if name == "gains" else ceil_to(rows[name], 16)
        self.shard = at
        self.node_part = self.off["edge_in"]
        self.piece = ceil_to(-(-at // n_sub), 16)
        self.total = self.piece * n_sub


def kernel(
    plan,
    node_ref,
    feat_ref,
    dst_ref,
    dir_ref,
    count_ref,
    wei_ref,
    weo_ref,
    wni_ref,
    wno_ref,
    gains_ref,
    ncot_ref,
    ecot_ref,
    node_out,
    edge_out,
    gei_out,
    geo_out,
    gni_out,
    gno_out,
    gain_out,
    wbuf,
    own,
    halo,
    strips,
    gstrips,
    ghalo,
    s_dst,
    s_src,
    t_dst,
    t_src,
    x_e,
    hid_e,
    normed_e,
    inv_e,
    gpre_e,
    graw_e,
    agg,
    x_n,
    g1,
    r1,
    p2,
    r2,
    fin,
    w_send,
    w_recv,
    h_send,
    h_recv,
    b_send,
    b_recv,
    n_send,
    n_recv,
    e_send,
    e_recv,
    q_send,
    q_recv,
    f_send,
    f_recv,
):
    n_dom, n_sub, side, edges = plan.n_dom, plan.n_sub, plan.side, plan.edges
    nodes, n_own, strip, lat = plan.nodes, plan.own, plan.strip, plan.latent
    n_halo, off, rows = plan.halo, plan.off, plan.rows
    d = lax.axis_index("dom")
    s = lax.axis_index("sub")

    halo[...] = jnp.zeros_like(halo)
    ghalo[...] = jnp.zeros_like(ghalo)
    barrier = pltpu.get_barrier_semaphore()
    for k in range(1, n_dom):
        pl.semaphore_signal(
            barrier, inc=1, device_id={"dom": lax.rem(d + k, n_dom)}, device_id_type=MESH
        )
    for k in range(1, n_sub):
        pl.semaphore_signal(
            barrier, inc=1, device_id={"sub": lax.rem(s + k, n_sub)}, device_id_type=MESH
        )

    shard_refs = {"edge_in": wei_ref, "edge_out": weo_ref, "node_in": wni_ref, "node_out": wno_ref}
    for name, ref in shard_refs.items():
        wbuf[d, off[name] : off[name] + rows[name], :] = ref[...]
    width = gains_ref.shape[1]
    gains32 = gains_ref[...].astype(F32)
    row16 = iota((16, width), 0)
    gains16 = jnp.where(
        row16 == 0, gains32[0:1, :], jnp.where(row16 == 1, gains32[1:2, :], 0.0)
    ).astype(BF)
    place = one_hot(iota((width, lat), 1) == iota((width, lat), 0) + d * width)
    wbuf[d, off["gains"] : off["gains"] + 16, :] = mm(gains16, place).astype(BF)

    own[0:nodes, :] = node_ref[...]
    own[nodes:n_own, :] = jnp.zeros((n_own - nodes, lat), BF)
    pos = iota((strip, n_own), 0)
    node_id = iota((strip, n_own), 1)
    inside = pos < side
    borders = (pos, (side - 1) * side + pos, pos * side, pos * side + side - 1)
    for b in range(4):
        select = one_hot((node_id == borders[b]) & inside)
        strips[b * strip : (b + 1) * strip, :] = mm(select, own[...]).astype(BF)

    pl.semaphore_wait(barrier, (n_dom - 1) + (n_sub - 1))

    w_copies = []
    for k in range(1, n_dom):
        copy = pltpu.make_async_remote_copy(
            src_ref=wbuf.at[d],
            dst_ref=wbuf.at[d],
            send_sem=w_send.at[k],
            recv_sem=w_recv.at[k],
            device_id={"dom": lax.rem(d + k, n_dom)},
            device_id_type=MESH,
        )
        copy.start()
        w_copies.append(copy)

    low_d, high_d = d > 0, d < n_dom - 1
    low_s, high_s = s > 0, s < n_sub - 1
    down_d, up_d = {"dom": jnp.maximum(d - 1, 0)}, {"dom": jnp.minimum(d + 1, n_dom - 1)}
    down_s, up_s = {"sub": jnp.maximum(s - 1, 0)}, {"sub": jnp.minimum(s + 1, n_sub - 1)}

    def strip_copies(source, target, send, recv, devices):
        return [
            pltpu.make_async_remote_copy(
                src_ref=source.at[pl.ds(b * strip, strip)],
                dst_ref=target.at[pl.ds(b * strip, strip)],
                send_sem=send.at[b],
                recv_sem=recv.at[b],
                device_id=devices[b],
                device_id_type=MESH,
            )
            for b in range(4)
        ]

    def when_all(conditions, actions):
        for condition, action in zip(conditions, actions):
            pl.when(condition)(action)

    h_copies = strip_copies(strips, halo, h_send, h_recv, (down_d, up_d, down_s, up_s))
    h_to, h_from = (low_d, high_d, low_s, high_s), (high_d, low_d, high_s, low_s)
    when_all(h_to, [c.start for c in h_copies])

    count = count_ref[0]
    for j in range(edges // LANES):
        at = j * LANES
        dst = dst_ref[j : j + 1, :]
        direction = dir_ref[j : j + 1, :]
        row = jnp.floor((dst.astype(F32) + 0.5) * (1.0 / side)).astype(jnp.int32)
        col = dst - row * side
        src = jnp.where(
            direction == 0,
            jnp.where(row == side - 1, n_own + col, dst + side),
            jnp.where(
                direction == 1,
                jnp.where(row == 0, n_own + strip + col, dst - side),
                jnp.where(
                    direction == 2,
                    jnp.where(col == side - 1, n_own + 2 * strip + row, dst + 1),
                    jnp.where(col == 0, n_own + 3 * strip + row, dst - 1),
                ),
            ),
        )
        dst = jnp.where(iota((1, LANES), 1) + at < count, dst, -1)
        dst_cols = jnp.broadcast_to(dst, (LANES, LANES)).T
        src_cols = jnp.broadcast_to(src, (LANES, LANES)).T
        lane = iota((LANES, LANES), 1)
        for t in range((n_own + n_halo) // LANES):
            cut = slice(t * LANES, (t + 1) * LANES)
            s_src[at : at + LANES, cut] = one_hot(src_cols == lane + t * LANES)
            if t < n_own // LANES:
                s_dst[at : at + LANES, cut] = one_hot(dst_cols == lane + t * LANES)
        t_src[:, at : at + LANES] = one_hot(iota((n_own + n_halo, LANES), 0) == src)
        t_dst[:, at : at + LANES] = one_hot(iota((n_own, LANES), 0) == dst)

    x_e[:, 0:lat] = feat_ref[...]
    chunks = split_rows(edges, 256)
    for at, size in chunks:
        x_e[at : at + size, 2 * lat :] = mm(s_dst[at : at + size, :], own[...]).astype(BF)
        x_e[at : at + size, lat : 2 * lat] = mm(
            s_src[at : at + size, 0:n_own], own[...]
        ).astype(BF)

    when_all(h_from, [c.wait_recv for c in h_copies])
    for at, size in chunks:
        far = mm(s_src[at : at + size, n_own:], halo[...])
        x_e[at : at + size, lat : 2 * lat] = (
            x_e[at : at + size, lat : 2 * lat].astype(F32) + far
        ).astype(BF)
    for copy in w_copies:
        copy.wait_recv()

    def whole(name):
        at, size = off[name], rows[name]
        if size % 16 == 0:
            return jnp.concatenate([wbuf[n, at : at + size, :] for n in range(n_dom)], axis=0)
        padded = ceil_to(size, 16)
        parts = [wbuf[n, at : at + padded, :].astype(F32)[0:size, :] for n in range(n_dom)]
        return jnp.concatenate(parts, axis=0).astype(BF)

    w1e, w2e, w1n, w2n = whole("edge_in"), whole("edge_out"), whole("node_in"), whole("node_out")
    gains = sum(wbuf[n, off["gains"] : off["gains"] + 16, :].astype(F32) for n in range(n_dom))
    gain_edge, gain_node = gains[0:1, :], gains[1:2, :]

    total = jnp.zeros((n_own, lat), F32)
    for at, size in chunks:
        hidden = jnp.maximum(mm(x_e[at : at + size, :], w1e), 0.0).astype(BF)
        hid_e[at : at + size, :] = hidden
        normed, inv_std = layer_norm(mm(hidden, w2e))
        normed_e[at : at + size, :] = normed
        inv_e[at : at + size, :] = inv_std
        message = normed * gain_edge
        high = message.astype(BF)
        low = (message - high.astype(F32)).astype(BF)
        both = mm(t_dst[:, at : at + size], jnp.concatenate([high, low], axis=1))
        total = total + both[:, 0:lat] + both[:, lat:]
    agg[...] = total.astype(BF)

    scale = (n_dom * n_sub * nodes) ** -0.5
    node_first = jnp.zeros((2 * lat, lat), F32)
    node_second = jnp.zeros((lat, lat), F32)
    node_gain = jnp.zeros((1, lat), F32)
    x_n[:, 0:lat] = own[...]
    x_n[:, lat:] = agg[...]
    node_grads = []
    for at, size in split_rows(nodes, 192):
        inputs = x_n[at : at + size, :]
        hidden = jnp.maximum(mm(inputs, w1n), 0.0).astype(BF)
        normed, inv_std = layer_norm(mm(hidden, w2n))
        upstream = ncot_ref[at : at + size, :].astype(F32)
        node_gain += jnp.sum(upstream * normed, axis=0, keepdims=True)
        graw = norm_back(upstream * gain_node, normed, inv_std).astype(BF)
        node_second += mm_tn(hidden, graw)
        gpre = jnp.where(hidden > 0, mm_nt(graw, w2n), 0.0).astype(BF)
        node_first += mm_tn(inputs, gpre)
        grad_in = mm_nt(gpre, w1n)
        node_grads.append(upstream + grad_in[:, 0:lat])
        agg[at : at + size, :] = grad_in[:, lat:].astype(BF)

    def pack(name, value):
        size = rows[name]
        for n in range(n_dom):
            g1[n, off[name] : off[name] + size, :] = (
                value[n * size : (n + 1) * size, :] * scale
            ).astype(BF)
            if size % 16:
                end = off[name] + ceil_to(size, 16)
                g1[n, off[name] + size : end, :] = jnp.zeros((end - off[name] - size, lat), BF)

    def dom_copies(first, last, send, recv):
        copies = []
        for k in range(1, n_dom):
            peer = lax.rem(d + k, n_dom)
            copy = pltpu.make_async_remote_copy(
                src_ref=g1.at[peer, pl.ds(first, last - first)],
                dst_ref=r1.at[k, pl.ds(first, last - first)],
                send_sem=send.at[k],
                recv_sem=recv.at[k],
                device_id={"dom": peer},
                device_id_type=MESH,
            )
            copy.start()
            copies.append(copy)
        return copies

    pack("node_in", node_first)
    pack("node_out", node_second)
    n_copies = dom_copies(0, plan.node_part, n_send, n_recv)

    edge_gain = jnp.zeros((1, lat), F32)
    for at, size in chunks:
        cot = ecot_ref[at : at + size, :].astype(F32)
        live = iota((size, lat), 0) + at < count
        upstream = jnp.where(live, cot, 0.0) + mm(s_dst[at : at + size, :], agg[...])
        normed, inv_std = normed_e[at : at + size, :], inv_e[at : at + size, :]
        edge_gain += jnp.sum(upstream * normed, axis=0, keepdims=True)
        graw = norm_back(upstream * gain_edge, normed, inv_std).astype(BF)
        graw_e[at : at + size, :] = graw
        gpre = jnp.where(hid_e[at : at + size, :] > 0, mm_nt(graw, w2e), 0.0).astype(BF)
        gpre_e[at : at + size, :] = gpre
        edge_out[at : at + size, :] = (cot + mm_nt(gpre, w1e[0:lat, :])).astype(BF)

    w_src, w_dst = w1e[lat : 2 * lat, :], w1e[2 * lat :, :]
    back = mm(t_src[n_own:, :], gpre_e[...]).astype(BF)
    gstrips[...] = mm_nt(back, w_src).astype(BF)
    b_copies = strip_copies(gstrips, ghalo, b_send, b_recv, (up_d, down_d, up_s, down_s))
    when_all(h_from, [c.start for c in b_copies])

    pack("edge_in", mm_tn(x_e[...], gpre_e[...]))
    pack("edge_out", mm_tn(hid_e[...], graw_e[...]))
    row16 = iota((16, lat), 0)
    gains16 = jnp.where(row16 == 0, edge_gain, jnp.where(row16 == 1, node_gain, 0.0))
    for n in range(n_dom):
        g1[n, off["gains"] : off["gains"] + 16, :] = (gains16 * scale).astype(BF)
        if plan.total > plan.shard:
            g1[n, plan.shard :, :] = jnp.zeros((plan.total - plan.shard, lat), BF)
    e_copies = dom_copies(plan.node_part, plan.total, e_send, e_recv)

    at_src = mm(t_src[0:n_own, :], gpre_e[...]).astype(BF)
    at_dst = mm(t_dst[...], gpre_e[...]).astype(BF)
    spread = mm_nt(at_src, w_src) + mm_nt(at_dst, w_dst)

    for copy in n_copies + e_copies:
        copy.wait_recv()
    acc = g1[d].astype(F32)
    for k in range(1, n_dom):
        acc = acc + r1[k].astype(F32)
    p2[...] = acc.astype(BF).reshape(n_sub, plan.piece, lat)
    q_copies = []
    for k in range(1, n_sub):
        peer = lax.rem(s + k, n_sub)
        copy = pltpu.make_async_remote_copy(
            src_ref=p2.at[peer],
            dst_ref=r2.at[k],
            send_sem=q_send.at[k],
            recv_sem=q_recv.at[k],
            device_id={"sub": peer},
            device_id_type=MESH,
        )
        copy.start()
        q_copies.append(copy)

    when_all(h_to, [c.wait_recv for c in b_copies])
    pos = iota((n_own, n_halo), 1)
    node_id = iota((n_own, n_halo), 0)
    picked = jnp.zeros((n_own, n_halo), jnp.bool_)
    for b in range(4):
        at = pos - b * strip
        border = (at, (side - 1) * side + at, at * side, at * side + side - 1)[b]
        picked = picked | ((at >= 0) & (at < side) & (node_id == border))
    spread = spread + mm(one_hot(picked), ghalo[...])
    for i, (at, size) in enumerate(split_rows(nodes, 192)):
        node_out[at : at + size, :] = (node_grads[i] + spread[at : at + size, :]).astype(BF)

    for copy in q_copies:
        copy.wait_recv()
    acc = p2[s].astype(F32)
    for k in range(1, n_sub):
        acc = acc + r2[k].astype(F32)
    fin[s] = acc.astype(BF)
    f_copies = []
    for k in range(1, n_sub):
        copy = pltpu.make_async_remote_copy(
            src_ref=fin.at[s],
            dst_ref=fin.at[s],
            send_sem=f_send.at[k],
            recv_sem=f_recv.at[k],
            device_id={"sub": lax.rem(s + k, n_sub)},
            device_id_type=MESH,
        )
        copy.start()
        f_copies.append(copy)
    for copy in f_copies:
        copy.wait_recv()
    result = fin[...].reshape(plan.total, lat)
    for name, ref in (
        ("edge_in", gei_out),
        ("edge_out", geo_out),
        ("node_in", gni_out),
        ("node_out", gno_out),
    ):
        ref[...] = result[off[name] : off[name] + ceil_to(rows[name], 16), :].astype(F32)[
            0 : rows[name], :
        ]
    gain_out[...] = mm_nt(result[off["gains"] : off["gains"] + 16, :], place)[0:2, :]

    for copy in w_copies + n_copies + e_copies + q_copies + f_copies:
        copy.wait_send()
    when_all(h_to, [c.wait_send for c in h_copies])
    when_all(h_from, [c.wait_send for c in b_copies])


def shards(
    node_feat,
    edge_feat,
    edge_dst,
    edge_dir,
    edge_count,
    w_edge_in,
    w_edge_out,
    w_node_in,
    w_node_out,
    gains,
    node_cot,
    edge_cot,
):
    n_dom, n_sub = lax.axis_size("dom"), lax.axis_size("sub")
    side, _, lat = node_feat.shape
    edges = edge_feat.shape[0]
    rows = {
        "edge_in": w_edge_in.shape[0],
        "edge_out": w_edge_out.shape[0],
        "node_in": w_node_in.shape[0],
        "node_out": w_node_out.shape[0],
    }
    plan = Plan(n_dom, n_sub, side, edges, lat, rows)
    nodes, n_own, n_halo = plan.nodes, plan.own, plan.halo
    vmem = pl.BlockSpec(memory_space=pltpu.VMEM)
    smem = pl.BlockSpec(memory_space=pltpu.SMEM)
    table = n_own + n_halo
    dma = pltpu.SemaphoreType.DMA
    outs = pl.pallas_call(
        functools.partial(kernel, plan),
        out_shape=[
            jax.ShapeDtypeStruct((nodes, lat), BF),
            jax.ShapeDtypeStruct((edges, lat), BF),
            jax.ShapeDtypeStruct(w_edge_in.shape, F32),
            jax.ShapeDtypeStruct(w_edge_out.shape, F32),
            jax.ShapeDtypeStruct(w_node_in.shape, F32),
            jax.ShapeDtypeStruct(w_node_out.shape, F32),
            jax.ShapeDtypeStruct(gains.shape, F32),
        ],
        in_specs=[vmem] * 4 + [smem] + [vmem] * 7,
        out_specs=[vmem] * 7,
        scratch_shapes=[
            pltpu.VMEM((n_dom, plan.shard, lat), BF),
            pltpu.VMEM((n_own, lat), BF),
            pltpu.VMEM((n_halo, lat), BF),
            pltpu.VMEM((n_halo, lat), BF),
            pltpu.VMEM((n_halo, lat), BF),
            pltpu.VMEM((n_halo, lat), BF),
            pltpu.VMEM((edges, n_own), BF),
            pltpu.VMEM((edges, table), BF),
            pltpu.VMEM((n_own, edges), BF),
            pltpu.VMEM((table, edges), BF),
            pltpu.VMEM((edges, 3 * lat), BF),
            pltpu.VMEM((edges, lat), BF),
            pltpu.VMEM((edges, lat), F32),
            pltpu.VMEM((edges, 1), F32),
            pltpu.VMEM((edges, lat), BF),
            pltpu.VMEM((edges, lat), BF),
            pltpu.VMEM((n_own, lat), BF),
            pltpu.VMEM((n_own, 2 * lat), BF),
            pltpu.VMEM((n_dom, plan.total, lat), BF),
            pltpu.VMEM((n_dom, plan.total, lat), BF),
            pltpu.VMEM((n_sub, plan.piece, lat), BF),
            pltpu.VMEM((n_sub, plan.piece, lat), BF),
            pltpu.VMEM((n_sub, plan.piece, lat), BF),
            dma((n_dom,)),
            dma((n_dom,)),
            dma((4,)),
            dma((4,)),
            dma((4,)),
            dma((4,)),
            dma((n_dom,)),
            dma((n_dom,)),
            dma((n_dom,)),
            dma((n_dom,)),
            dma((n_sub,)),
            dma((n_sub,)),
            dma((n_sub,)),
            dma((n_sub,)),
        ],
        compiler_params=pltpu.CompilerParams(
            collective_id=0, has_side_effects=True, vmem_limit_bytes=48 * 1024 * 1024
        ),
        name="graph_layer_backward",
    )(
        node_feat.reshape(nodes, lat),
        edge_feat,
        edge_dst.reshape(edges // LANES, LANES),
        edge_dir.reshape(edges // LANES, LANES),
        edge_count,
        w_edge_in,
        w_edge_out,
        w_node_in,
        w_node_out,
        gains,
        node_cot.reshape(nodes, lat),
        edge_cot,
    )
    return (outs[0].reshape(node_feat.shape), *outs[1:])


def solution(mesh):
    in_specs = (
        P("dom", "sub", None),
        P(("dom", "sub"), None),
        P(("dom", "sub")),
        P(("dom", "sub")),
        P(("dom", "sub")),
        P("dom", None),
        P("dom", None),
        P("dom", None),
        P("dom", None),
        P(None, "dom"),
        P("dom", "sub", None),
        P(("dom", "sub"), None),
    )
    out_specs = (
        P("dom", "sub", None),
        P(("dom", "sub"), None),
        P("dom", None),
        P("dom", None),
        P("dom", None),
        P("dom", None),
        P(None, "dom"),
    )
    return jax.shard_map(shards, mesh=mesh, in_specs=in_specs, out_specs=out_specs, check_vma=False)
```

```python
import functools

import jax
import jax.numpy as jnp
from jax import lax
from jax.experimental import pallas as pl
from jax.experimental.pallas import tpu as pltpu
from jax.sharding import PartitionSpec as P

MESH = pl.DeviceIdType.MESH
BF = jnp.bfloat16
F32 = jnp.float32
LANES = 128


def ceil_to(value, step):
    return -(-value // step) * step


def mm(a, b):
    return jnp.dot(a, b, preferred_element_type=F32)


def mm_nt(a, b):
    return lax.dot_general(a, b, (((1,), (1,)), ((), ())), preferred_element_type=F32)


def mm_tn(a, b):
    return lax.dot_general(a, b, (((0,), (0,)), ((), ())), preferred_element_type=F32)


def iota(shape, dim):
    return lax.broadcasted_iota(jnp.int32, shape, dim)


def one_hot(mask):
    return jnp.where(mask, 1.0, 0.0).astype(BF)


def layer_norm(raw_out):
    average = jnp.mean(raw_out, axis=-1, keepdims=True)
    centered = raw_out - average
    inv_std = lax.rsqrt(jnp.mean(centered * centered, axis=-1, keepdims=True) + 1e-05)
    return centered * inv_std, inv_std


def norm_back(upstream, normed, inv_std):
    return (
        upstream
        - jnp.mean(upstream, axis=-1, keepdims=True)
        - normed * jnp.mean(upstream * normed, axis=-1, keepdims=True)
    ) * inv_std


def split_rows(total, step):
    return [(at, min(step, total - at)) for at in range(0, total, step)]


class Plan:
    def __init__(self, n_dom, n_sub, side, edges, latent, rows):
        self.n_dom, self.n_sub = n_dom, n_sub
        self.side, self.edges, self.latent = side, edges, latent
        self.nodes = side * side
        self.own = ceil_to(self.nodes, LANES)
        self.strip = ceil_to(side, 16)
        self.halo = ceil_to(4 * self.strip, LANES)
        self.rows = rows
        at = 0
        self.off = {}
        for name in ("node_in", "node_out", "edge_in", "edge_out", "gains"):
            self.off[name] = at
            at += 16 if name == "gains" else ceil_to(rows[name], 16)
        self.shard = at
        self.node_part = self.off["edge_in"]
        self.piece = ceil_to(-(-at // n_sub), 16)
        self.total = self.piece * n_sub


def kernel(
    plan,
    node_hbm,
    feat_hbm,
    dst_hbm,
    dir_hbm,
    count_ref,
    wei_hbm,
    weo_hbm,
    wni_hbm,
    wno_hbm,
    gains_hbm,
    ncot_hbm,
    ecot_hbm,
    node_out_hbm,
    edge_out_hbm,
    gei_out_hbm,
    geo_out_hbm,
    gni_out_hbm,
    gno_out_hbm,
    gain_out_hbm,
    node_out,
    edge_out,
    gei_out,
    geo_out,
    gni_out,
    gno_out,
    gain_out,
    out_sem,
    node_ref,
    feat_ref,
    dst_ref,
    dir_ref,
    wei_ref,
    weo_ref,
    wni_ref,
    wno_ref,
    gains_ref,
    ncot_ref,
    ecot_ref,
    in_sem,
    wbuf,
    own,
    halo,
    strips,
    gstrips,
    ghalo,
    s_dst,
    s_src,
    t_dst,
    t_src,
    x_e,
    hid_e,
    normed_e,
    inv_e,
    gpre_e,
    graw_e,
    msg,
    agg,
    x_n,
    g1,
    r1,
    p2,
    r2,
    fin,
    w_send,
    w_recv,
    h_send,
    h_recv,
    b_send,
    b_recv,
    n_send,
    n_recv,
    e_send,
    e_recv,
    q_send,
    q_recv,
    f_send,
    f_recv,
):
    n_dom, n_sub, side, edges = plan.n_dom, plan.n_sub, plan.side, plan.edges
    nodes, n_own, strip, lat = plan.nodes, plan.own, plan.strip, plan.latent
    n_halo, off, rows = plan.halo, plan.off, plan.rows
    d = lax.axis_index("dom")
    s = lax.axis_index("sub")

    pairs = (
        (wei_hbm, wei_ref),
        (weo_hbm, weo_ref),
        (wni_hbm, wni_ref),
        (wno_hbm, wno_ref),
        (gains_hbm, gains_ref),
        (node_hbm, node_ref),
        (dst_hbm, dst_ref),
        (dir_hbm, dir_ref),
        (feat_hbm, feat_ref),
        (ncot_hbm, ncot_ref),
        (ecot_hbm, ecot_ref),
    )
    loads = [
        pltpu.make_async_copy(hbm, ref, in_sem.at[i]) for i, (hbm, ref) in enumerate(pairs)
    ]
    for load in loads:
        load.start()
    pairs = (
        (node_out, node_out_hbm),
        (edge_out, edge_out_hbm),
        (gei_out, gei_out_hbm),
        (geo_out, geo_out_hbm),
        (gni_out, gni_out_hbm),
        (gno_out, gno_out_hbm),
        (gain_out, gain_out_hbm),
    )
    stores = [
        pltpu.make_async_copy(ref, hbm, out_sem.at[i]) for i, (ref, hbm) in enumerate(pairs)
    ]

    halo[...] = jnp.zeros_like(halo)
    ghalo[...] = jnp.zeros_like(ghalo)
    barrier = pltpu.get_barrier_semaphore()
    for k in range(1, n_dom):
        pl.semaphore_signal(
            barrier, inc=1, device_id={"dom": lax.rem(d + k, n_dom)}, device_id_type=MESH
        )
    for k in range(1, n_sub):
        pl.semaphore_signal(
            barrier, inc=1, device_id={"sub": lax.rem(s + k, n_sub)}, device_id_type=MESH
        )

    for load in loads[:5]:
        load.wait()
    shard_refs = {"edge_in": wei_ref, "edge_out": weo_ref, "node_in": wni_ref, "node_out": wno_ref}
    for name, ref in shard_refs.items():
        wbuf[d, off[name] : off[name] + rows[name], :] = ref[...]
    width = gains_ref.shape[1]
    gains32 = gains_ref[...].astype(F32)
    row16 = iota((16, width), 0)
    gains16 = jnp.where(
        row16 == 0, gains32[0:1, :], jnp.where(row16 == 1, gains32[1:2, :], 0.0)
    ).astype(BF)
    place = one_hot(iota((width, lat), 1) == iota((width, lat), 0) + d * width)
    wbuf[d, off["gains"] : off["gains"] + 16, :] = mm(gains16, place).astype(BF)

    loads[5].wait()
    own[0:nodes, :] = node_ref[...]
    own[nodes:n_own, :] = jnp.zeros((n_own - nodes, lat), BF)
    pos = iota((strip, n_own), 0)
    node_id = iota((strip, n_own), 1)
    inside = pos < side
    borders = (pos, (side - 1) * side + pos, pos * side, pos * side + side - 1)
    for b in range(4):
        select = one_hot((node_id == borders[b]) & inside)
        strips[b * strip : (b + 1) * strip, :] = mm(select, own[...]).astype(BF)

    pl.semaphore_wait(barrier, (n_dom - 1) + (n_sub - 1))

    w_copies = []
    for k in range(1, n_dom):
        copy = pltpu.make_async_remote_copy(
            src_ref=wbuf.at[d],
            dst_ref=wbuf.at[d],
            send_sem=w_send.at[k],
            recv_sem=w_recv.at[k],
            device_id={"dom": lax.rem(d + k, n_dom)},
            device_id_type=MESH,
        )
        copy.start()
        w_copies.append(copy)

    low_d, high_d = d > 0, d < n_dom - 1
    low_s, high_s = s > 0, s < n_sub - 1
    down_d, up_d = {"dom": jnp.maximum(d - 1, 0)}, {"dom": jnp.minimum(d + 1, n_dom - 1)}
    down_s, up_s = {"sub": jnp.maximum(s - 1, 0)}, {"sub": jnp.minimum(s + 1, n_sub - 1)}

    def strip_copies(source, target, send, recv, devices):
        return [
            pltpu.make_async_remote_copy(
                src_ref=source.at[pl.ds(b * strip, strip)],
                dst_ref=target.at[pl.ds(b * strip, strip)],
                send_sem=send.at[b],
                recv_sem=recv.at[b],
                device_id=devices[b],
                device_id_type=MESH,
            )
            for b in range(4)
        ]

    def when_all(conditions, actions):
        for condition, action in zip(conditions, actions):
            pl.when(condition)(action)

    h_copies = strip_copies(strips, halo, h_send, h_recv, (down_d, up_d, down_s, up_s))
    h_to, h_from = (low_d, high_d, low_s, high_s), (high_d, low_d, high_s, low_s)
    when_all(h_to, [c.start for c in h_copies])

    for load in loads[6:9]:
        load.wait()
    count = count_ref[0]
    for j in range(edges // LANES):
        at = j * LANES
        dst = dst_ref[j : j + 1, :]
        direction = dir_ref[j : j + 1, :]
        row = jnp.floor((dst.astype(F32) + 0.5) * (1.0 / side)).astype(jnp.int32)
        col = dst - row * side
        src = jnp.where(
            direction == 0,
            jnp.where(row == side - 1, n_own + col, dst + side),
            jnp.where(
                direction == 1,
                jnp.where(row == 0, n_own + strip + col, dst - side),
                jnp.where(
                    direction == 2,
                    jnp.where(col == side - 1, n_own + 2 * strip + row, dst + 1),
                    jnp.where(col == 0, n_own + 3 * strip + row, dst - 1),
                ),
            ),
        )
        dst = jnp.where(iota((1, LANES), 1) + at < count, dst, -1)
        dst_cols = jnp.broadcast_to(dst, (LANES, LANES)).T
        src_cols = jnp.broadcast_to(src, (LANES, LANES)).T
        lane = iota((LANES, LANES), 1)
        for t in range((n_own + n_halo) // LANES):
            cut = slice(t * LANES, (t + 1) * LANES)
            s_src[at : at + LANES, cut] = one_hot(src_cols == lane + t * LANES)
            if t < n_own // LANES:
                s_dst[at : at + LANES, cut] = one_hot(dst_cols == lane + t * LANES)
        t_src[:, at : at + LANES] = one_hot(iota((n_own + n_halo, LANES), 0) == src)
        t_dst[:, at : at + LANES] = one_hot(iota((n_own, LANES), 0) == dst)

    x_e[:, 0:lat] = feat_ref[...]
    chunks = split_rows(edges, 256)
    for at, size in chunks:
        x_e[at : at + size, 2 * lat :] = mm(s_dst[at : at + size, :], own[...]).astype(BF)
        x_e[at : at + size, lat : 2 * lat] = mm(
            s_src[at : at + size, 0:n_own], own[...]
        ).astype(BF)

    when_all(h_from, [c.wait_recv for c in h_copies])
    for at, size in chunks:
        far = mm(s_src[at : at + size, n_own:], halo[...])
        x_e[at : at + size, lat : 2 * lat] = (
            x_e[at : at + size, lat : 2 * lat].astype(F32) + far
        ).astype(BF)
    for copy in w_copies:
        copy.wait_recv()

    def whole(name):
        at, size = off[name], rows[name]
        if size % 16 == 0:
            return jnp.concatenate([wbuf[n, at : at + size, :] for n in range(n_dom)], axis=0)
        padded = ceil_to(size, 16)
        parts = [wbuf[n, at : at + padded, :].astype(F32)[0:size, :] for n in range(n_dom)]
        return jnp.concatenate(parts, axis=0).astype(BF)

    w1e, w2e, w1n, w2n = whole("edge_in"), whole("edge_out"), whole("node_in"), whole("node_out")
    gains = sum(wbuf[n, off["gains"] : off["gains"] + 16, :].astype(F32) for n in range(n_dom))
    gain_edge, gain_node = gains[0:1, :], gains[1:2, :]

    for at, size in chunks:
        hidden = jnp.maximum(mm(x_e[at : at + size, :], w1e), 0.0).astype(BF)
        hid_e[at : at + size, :] = hidden
        normed, inv_std = layer_norm(mm(hidden, w2e))
        normed_e[at : at + size, :] = normed
        inv_e[at : at + size, :] = inv_std
        message = normed * gain_edge
        high = message.astype(BF)
        msg[at : at + size, 0:lat] = high
        msg[at : at + size, lat:] = (message - high.astype(F32)).astype(BF)
    both = mm(t_dst[...], msg[...])
    agg[...] = (both[:, 0:lat] + both[:, lat:]).astype(BF)

    for load in loads[9:]:
        load.wait()
    scale = (n_dom * n_sub * nodes) ** -0.5
    node_first = jnp.zeros((2 * lat, lat), F32)
    node_second = jnp.zeros((lat, lat), F32)
    node_gain = jnp.zeros((1, lat), F32)
    x_n[:, 0:lat] = own[...]
    x_n[:, lat:] = agg[...]
    node_grads = []
    for at, size in split_rows(nodes, 192):
        inputs = x_n[at : at + size, :]
        hidden = jnp.maximum(mm(inputs, w1n), 0.0).astype(BF)
        normed, inv_std = layer_norm(mm(hidden, w2n))
        upstream = ncot_ref[at : at + size, :].astype(F32)
        node_gain += jnp.sum(upstream * normed, axis=0, keepdims=True)
        graw = norm_back(upstream * gain_node, normed, inv_std).astype(BF)
        node_second += mm_tn(hidden, graw)
        gpre = jnp.where(hidden > 0, mm_nt(graw, w2n), 0.0).astype(BF)
        node_first += mm_tn(inputs, gpre)
        grad_in = mm_nt(gpre, w1n)
        node_grads.append(upstream + grad_in[:, 0:lat])
        agg[at : at + size, :] = grad_in[:, lat:].astype(BF)

    def pack(name, value):
        size = rows[name]
        for n in range(n_dom):
            g1[n, off[name] : off[name] + size, :] = (
                value[n * size : (n + 1) * size, :] * scale
            ).astype(BF)
            if size % 16:
                end = off[name] + ceil_to(size, 16)
                g1[n, off[name] + size : end, :] = jnp.zeros((end - off[name] - size, lat), BF)

    def dom_copies(first, last, send, recv):
        copies = []
        for k in range(1, n_dom):
            peer = lax.rem(d + k, n_dom)
            copy = pltpu.make_async_remote_copy(
                src_ref=g1.at[peer, pl.ds(first, last - first)],
                dst_ref=r1.at[k, pl.ds(first, last - first)],
                send_sem=send.at[k],
                recv_sem=recv.at[k],
                device_id={"dom": peer},
                device_id_type=MESH,
            )
            copy.start()
            copies.append(copy)
        return copies

    pack("node_in", node_first)
    pack("node_out", node_second)
    n_copies = dom_copies(0, plan.node_part, n_send, n_recv)

    edge_gain = jnp.zeros((1, lat), F32)
    for at, size in chunks:
        cot = ecot_ref[at : at + size, :].astype(F32)
        live = iota((size, lat), 0) + at < count
        upstream = jnp.where(live, cot, 0.0) + mm(s_dst[at : at + size, :], agg[...])
        normed, inv_std = normed_e[at : at + size, :], inv_e[at : at + size, :]
        edge_gain += jnp.sum(upstream * normed, axis=0, keepdims=True)
        graw = norm_back(upstream * gain_edge, normed, inv_std).astype(BF)
        graw_e[at : at + size, :] = graw
        gpre = jnp.where(hid_e[at : at + size, :] > 0, mm_nt(graw, w2e), 0.0).astype(BF)
        gpre_e[at : at + size, :] = gpre

    pack("edge_in", mm_tn(x_e[...], gpre_e[...]))
    pack("edge_out", mm_tn(hid_e[...], graw_e[...]))
    row16 = iota((16, lat), 0)
    gains16 = jnp.where(row16 == 0, edge_gain, jnp.where(row16 == 1, node_gain, 0.0))
    for n in range(n_dom):
        g1[n, off["gains"] : off["gains"] + 16, :] = (gains16 * scale).astype(BF)
        if plan.total > plan.shard:
            g1[n, plan.shard :, :] = jnp.zeros((plan.total - plan.shard, lat), BF)
    e_copies = dom_copies(plan.node_part, plan.total, e_send, e_recv)

    w_src, w_dst = w1e[lat : 2 * lat, :], w1e[2 * lat :, :]
    back = mm(t_src[n_own:, :], gpre_e[...]).astype(BF)
    gstrips[...] = mm_nt(back, w_src).astype(BF)
    b_copies = strip_copies(gstrips, ghalo, b_send, b_recv, (up_d, down_d, up_s, down_s))
    when_all(h_from, [c.start for c in b_copies])

    for at, size in chunks:
        cot = ecot_ref[at : at + size, :].astype(F32)
        grad = mm_nt(gpre_e[at : at + size, :], w1e[0:lat, :])
        edge_out[at : at + size, :] = (cot + grad).astype(BF)
    stores[1].start()

    at_src = mm(t_src[0:n_own, :], gpre_e[...]).astype(BF)
    at_dst = mm(t_dst[...], gpre_e[...]).astype(BF)
    spread = mm_nt(at_src, w_src) + mm_nt(at_dst, w_dst)

    for copy in n_copies + e_copies:
        copy.wait_recv()
    acc = g1[d].astype(F32)
    for k in range(1, n_dom):
        acc = acc + r1[k].astype(F32)
    p2[...] = acc.astype(BF).reshape(n_sub, plan.piece, lat)
    q_copies = []
    for k in range(1, n_sub):
        peer = lax.rem(s + k, n_sub)
        copy = pltpu.make_async_remote_copy(
            src_ref=p2.at[peer],
            dst_ref=r2.at[k],
            send_sem=q_send.at[k],
            recv_sem=q_recv.at[k],
            device_id={"sub": peer},
            device_id_type=MESH,
        )
        copy.start()
        q_copies.append(copy)

    when_all(h_to, [c.wait_recv for c in b_copies])
    pos = iota((n_own, n_halo), 1)
    node_id = iota((n_own, n_halo), 0)
    picked = jnp.zeros((n_own, n_halo), jnp.bool_)
    for b in range(4):
        at = pos - b * strip
        border = (at, (side - 1) * side + at, at * side, at * side + side - 1)[b]
        picked = picked | ((at >= 0) & (at < side) & (node_id == border))
    spread = spread + mm(one_hot(picked), ghalo[...])
    for i, (at, size) in enumerate(split_rows(nodes, 192)):
        node_out[at : at + size, :] = (node_grads[i] + spread[at : at + size, :]).astype(BF)
    stores[0].start()

    for copy in q_copies:
        copy.wait_recv()
    acc = p2[s].astype(F32)
    for k in range(1, n_sub):
        acc = acc + r2[k].astype(F32)
    fin[s] = acc.astype(BF)
    f_copies = []
    for k in range(1, n_sub):
        copy = pltpu.make_async_remote_copy(
            src_ref=fin.at[s],
            dst_ref=fin.at[s],
            send_sem=f_send.at[k],
            recv_sem=f_recv.at[k],
            device_id={"sub": lax.rem(s + k, n_sub)},
            device_id_type=MESH,
        )
        copy.start()
        f_copies.append(copy)
    for copy in f_copies:
        copy.wait_recv()
    result = fin[...].reshape(plan.total, lat)
    for name, ref in (
        ("edge_in", gei_out),
        ("edge_out", geo_out),
        ("node_in", gni_out),
        ("node_out", gno_out),
    ):
        ref[...] = result[off[name] : off[name] + ceil_to(rows[name], 16), :].astype(F32)[
            0 : rows[name], :
        ]
    gain_out[...] = mm_nt(result[off["gains"] : off["gains"] + 16, :], place)[0:2, :]
    for store in stores[2:]:
        store.start()

    for copy in w_copies + n_copies + e_copies + q_copies + f_copies:
        copy.wait_send()
    when_all(h_to, [c.wait_send for c in h_copies])
    when_all(h_from, [c.wait_send for c in b_copies])
    for store in stores:
        store.wait()


def write_out(*refs):
    sources, targets, sem = refs[:7], refs[7:14], refs[14]
    copies = [
        pltpu.make_async_copy(a, b, sem.at[i]) for i, (a, b) in enumerate(zip(sources, targets))
    ]
    for copy in copies:
        copy.start()
    for copy in copies:
        copy.wait()


def shards(
    node_feat,
    edge_feat,
    edge_dst,
    edge_dir,
    edge_count,
    w_edge_in,
    w_edge_out,
    w_node_in,
    w_node_out,
    gains,
    node_cot,
    edge_cot,
):
    n_dom, n_sub = lax.axis_size("dom"), lax.axis_size("sub")
    side, _, lat = node_feat.shape
    edges = edge_feat.shape[0]
    rows = {
        "edge_in": w_edge_in.shape[0],
        "edge_out": w_edge_out.shape[0],
        "node_in": w_node_in.shape[0],
        "node_out": w_node_out.shape[0],
    }
    plan = Plan(n_dom, n_sub, side, edges, lat, rows)
    nodes, n_own, n_halo = plan.nodes, plan.own, plan.halo
    table = n_own + n_halo
    dma = pltpu.SemaphoreType.DMA
    hbm = pl.BlockSpec(memory_space=pltpu.HBM)
    vmem_limit = 64 * 1024 * 1024
    out_shape = [
        jax.ShapeDtypeStruct((nodes, lat), BF),
        jax.ShapeDtypeStruct((edges, lat), BF),
        jax.ShapeDtypeStruct(w_edge_in.shape, F32),
        jax.ShapeDtypeStruct(w_edge_out.shape, F32),
        jax.ShapeDtypeStruct(w_node_in.shape, F32),
        jax.ShapeDtypeStruct(w_node_out.shape, F32),
        jax.ShapeDtypeStruct(gains.shape, F32),
    ]
    outs = pl.pallas_call(
        functools.partial(kernel, plan),
        out_shape=out_shape,
        in_specs=[hbm] * 4 + [pl.BlockSpec(memory_space=pltpu.SMEM)] + [hbm] * 7,
        out_specs=[hbm] * 7,
        scratch_shapes=[pltpu.VMEM(out.shape, out.dtype) for out in out_shape]
        + [
            dma((7,)),
            pltpu.VMEM((nodes, lat), BF),
            pltpu.VMEM((edges, lat), BF),
            pltpu.VMEM((edges // LANES, LANES), jnp.int32),
            pltpu.VMEM((edges // LANES, LANES), jnp.int32),
            pltpu.VMEM(w_edge_in.shape, BF),
            pltpu.VMEM(w_edge_out.shape, BF),
            pltpu.VMEM(w_node_in.shape, BF),
            pltpu.VMEM(w_node_out.shape, BF),
            pltpu.VMEM(gains.shape, BF),
            pltpu.VMEM((nodes, lat), BF),
            pltpu.VMEM((edges, lat), BF),
            dma((11,)),
            pltpu.VMEM((n_dom, plan.shard, lat), BF),
            pltpu.VMEM((n_own, lat), BF),
            pltpu.VMEM((n_halo, lat), BF),
            pltpu.VMEM((n_halo, lat), BF),
            pltpu.VMEM((n_halo, lat), BF),
            pltpu.VMEM((n_halo, lat), BF),
            pltpu.VMEM((edges, n_own), BF),
            pltpu.VMEM((edges, table), BF),
            pltpu.VMEM((n_own, edges), BF),
            pltpu.VMEM((table, edges), BF),
            pltpu.VMEM((edges, 3 * lat), BF),
            pltpu.VMEM((edges, lat), BF),
            pltpu.VMEM((edges, lat), F32),
            pltpu.VMEM((edges, 1), F32),
            pltpu.VMEM((edges, lat), BF),
            pltpu.VMEM((edges, lat), BF),
            pltpu.VMEM((edges, 2 * lat), BF),
            pltpu.VMEM((n_own, lat), BF),
            pltpu.VMEM((n_own, 2 * lat), BF),
            pltpu.VMEM((n_dom, plan.total, lat), BF),
            pltpu.VMEM((n_dom, plan.total, lat), BF),
            pltpu.VMEM((n_sub, plan.piece, lat), BF),
            pltpu.VMEM((n_sub, plan.piece, lat), BF),
            pltpu.VMEM((n_sub, plan.piece, lat), BF),
            dma((n_dom,)),
            dma((n_dom,)),
            dma((4,)),
            dma((4,)),
            dma((4,)),
            dma((4,)),
            dma((n_dom,)),
            dma((n_dom,)),
            dma((n_dom,)),
            dma((n_dom,)),
            dma((n_sub,)),
            dma((n_sub,)),
            dma((n_sub,)),
            dma((n_sub,)),
        ],
        compiler_params=pltpu.CompilerParams(
            collective_id=0, has_side_effects=True, vmem_limit_bytes=vmem_limit
        ),
        name="graph_layer_backward",
    )(
        node_feat.reshape(nodes, lat),
        edge_feat,
        edge_dst.reshape(edges // LANES, LANES),
        edge_dir.reshape(edges // LANES, LANES),
        edge_count,
        w_edge_in,
        w_edge_out,
        w_node_in,
        w_node_out,
        gains,
        node_cot.reshape(nodes, lat),
        edge_cot,
    )
    outs = pl.pallas_call(
        write_out,
        out_shape=out_shape,
        in_specs=[hbm] * 7,
        out_specs=[hbm] * 7,
        scratch_shapes=[dma((7,))],
        compiler_params=pltpu.CompilerParams(vmem_limit_bytes=vmem_limit),
        name="write_results",
    )(*outs)
    return (outs[0].reshape(node_feat.shape), *outs[1:])


def solution(mesh):
    in_specs = (
        P("dom", "sub", None),
        P(("dom", "sub"), None),
        P(("dom", "sub")),
        P(("dom", "sub")),
        P(("dom", "sub")),
        P("dom", None),
        P("dom", None),
        P("dom", None),
        P("dom", None),
        P(None, "dom"),
        P("dom", "sub", None),
        P(("dom", "sub"), None),
    )
    out_specs = (
        P("dom", "sub", None),
        P(("dom", "sub"), None),
        P("dom", None),
        P("dom", None),
        P("dom", None),
        P("dom", None),
        P(None, "dom"),
    )
    return jax.shard_map(shards, mesh=mesh, in_specs=in_specs, out_specs=out_specs, check_vma=False)
```

```python
import functools

import jax
import jax.numpy as jnp
from jax import lax
from jax.experimental import pallas as pl
from jax.experimental.pallas import tpu as pltpu
from jax.sharding import PartitionSpec as P

MESH = pl.DeviceIdType.MESH
BF = jnp.bfloat16
F32 = jnp.float32
LANES = 128


def ceil_to(value, step):
    return -(-value // step) * step


def mm(a, b):
    return jnp.dot(a, b, preferred_element_type=F32)


def mm_nt(a, b):
    return lax.dot_general(a, b, (((1,), (1,)), ((), ())), preferred_element_type=F32)


def mm_tn(a, b):
    return lax.dot_general(a, b, (((0,), (0,)), ((), ())), preferred_element_type=F32)


def iota(shape, dim):
    return lax.broadcasted_iota(jnp.int32, shape, dim)


def one_hot(mask):
    return jnp.where(mask, 1.0, 0.0).astype(BF)


def layer_norm(raw_out):
    average = jnp.mean(raw_out, axis=-1, keepdims=True)
    centered = raw_out - average
    inv_std = lax.rsqrt(jnp.mean(centered * centered, axis=-1, keepdims=True) + 1e-05)
    return centered * inv_std, inv_std


def norm_back(upstream, normed, inv_std):
    return (
        upstream
        - jnp.mean(upstream, axis=-1, keepdims=True)
        - normed * jnp.mean(upstream * normed, axis=-1, keepdims=True)
    ) * inv_std


def each_chunk(total, step, body, init=0):
    def turn(i, carry):
        at = pl.multiple_of(i * step, step)
        return body(pl.ds(at, step), at, carry)

    return lax.fori_loop(0, total // step, turn, init)


class Plan:
    def __init__(self, n_dom, n_sub, side, edges, latent, rows):
        self.n_dom, self.n_sub = n_dom, n_sub
        self.side, self.edges, self.latent = side, edges, latent
        self.nodes = side * side
        self.own = ceil_to(self.nodes, LANES)
        self.strip = ceil_to(side, 16)
        self.halo = ceil_to(4 * self.strip, LANES)
        self.rows = rows
        at = 0
        self.off = {}
        for name in ("node_in", "node_out", "edge_in", "edge_out", "gains"):
            self.off[name] = at
            at += 16 if name == "gains" else ceil_to(rows[name], 16)
        self.shard = at
        self.node_part = self.off["edge_in"]
        self.piece = ceil_to(-(-at // n_sub), 16)
        self.total = self.piece * n_sub


def kernel(
    plan,
    node_hbm,
    feat_hbm,
    dst_hbm,
    dir_hbm,
    count_ref,
    wei_hbm,
    weo_hbm,
    wni_hbm,
    wno_hbm,
    gains_hbm,
    ncot_hbm,
    ecot_hbm,
    node_out_hbm,
    edge_out_hbm,
    gei_out_hbm,
    geo_out_hbm,
    gni_out_hbm,
    gno_out_hbm,
    gain_out_hbm,
    node_out,
    edge_out,
    gei_out,
    geo_out,
    gni_out,
    gno_out,
    gain_out,
    out_sem,
    node_ref,
    feat_ref,
    dst_ref,
    dir_ref,
    wei_ref,
    weo_ref,
    wni_ref,
    wno_ref,
    gains_ref,
    ncot_ref,
    ecot_ref,
    in_sem,
    wbuf,
    own,
    halo,
    strips,
    gstrips,
    ghalo,
    s_dst,
    s_src,
    t_dst,
    t_src,
    x_e,
    hid_e,
    normed_e,
    inv_e,
    gpre_e,
    graw_e,
    msg,
    agg,
    x_n,
    hid_n,
    graw_n,
    gpre_n,
    node_acc,
    g1,
    r1,
    p2,
    r2,
    fin,
    w_send,
    w_recv,
    h_send,
    h_recv,
    b_send,
    b_recv,
    n_send,
    n_recv,
    e_send,
    e_recv,
    q_send,
    q_recv,
    f_send,
    f_recv,
):
    n_dom, n_sub, side, edges = plan.n_dom, plan.n_sub, plan.side, plan.edges
    nodes, n_own, strip, lat = plan.nodes, plan.own, plan.strip, plan.latent
    n_halo, off, rows = plan.halo, plan.off, plan.rows
    d = lax.axis_index("dom")
    s = lax.axis_index("sub")

    pairs = (
        (wei_hbm, wei_ref),
        (weo_hbm, weo_ref),
        (wni_hbm, wni_ref),
        (wno_hbm, wno_ref),
        (gains_hbm, gains_ref),
        (node_hbm, node_ref),
        (dst_hbm, dst_ref),
        (dir_hbm, dir_ref),
        (feat_hbm, feat_ref),
        (ncot_hbm, ncot_ref),
        (ecot_hbm, ecot_ref),
    )
    loads = [
        pltpu.make_async_copy(hbm, ref, in_sem.at[i]) for i, (hbm, ref) in enumerate(pairs)
    ]
    for load in loads:
        load.start()
    pairs = (
        (node_out, node_out_hbm),
        (edge_out, edge_out_hbm),
        (gei_out, gei_out_hbm),
        (geo_out, geo_out_hbm),
        (gni_out, gni_out_hbm),
        (gno_out, gno_out_hbm),
        (gain_out, gain_out_hbm),
    )
    stores = [
        pltpu.make_async_copy(ref, hbm, out_sem.at[i]) for i, (ref, hbm) in enumerate(pairs)
    ]

    halo[...] = jnp.zeros_like(halo)
    ghalo[...] = jnp.zeros_like(ghalo)
    barrier = pltpu.get_barrier_semaphore()
    for k in range(1, n_dom):
        pl.semaphore_signal(
            barrier, inc=1, device_id={"dom": lax.rem(d + k, n_dom)}, device_id_type=MESH
        )
    for k in range(1, n_sub):
        pl.semaphore_signal(
            barrier, inc=1, device_id={"sub": lax.rem(s + k, n_sub)}, device_id_type=MESH
        )

    for load in loads[:5]:
        load.wait()
    shard_refs = {"edge_in": wei_ref, "edge_out": weo_ref, "node_in": wni_ref, "node_out": wno_ref}
    for name, ref in shard_refs.items():
        wbuf[d, off[name] : off[name] + rows[name], :] = ref[...]
    width = gains_ref.shape[1]
    gains32 = gains_ref[...].astype(F32)
    row16 = iota((16, width), 0)
    gains16 = jnp.where(
        row16 == 0, gains32[0:1, :], jnp.where(row16 == 1, gains32[1:2, :], 0.0)
    ).astype(BF)
    place = one_hot(iota((width, lat), 1) == iota((width, lat), 0) + d * width)
    wbuf[d, off["gains"] : off["gains"] + 16, :] = mm(gains16, place).astype(BF)

    loads[5].wait()
    own[0:nodes, :] = node_ref[...]
    own[nodes:n_own, :] = jnp.zeros((n_own - nodes, lat), BF)
    pos = iota((strip, n_own), 0)
    node_id = iota((strip, n_own), 1)
    inside = pos < side
    borders = (pos, (side - 1) * side + pos, pos * side, pos * side + side - 1)
    for b in range(4):
        select = one_hot((node_id == borders[b]) & inside)
        strips[b * strip : (b + 1) * strip, :] = mm(select, own[...]).astype(BF)

    pl.semaphore_wait(barrier, (n_dom - 1) + (n_sub - 1))

    w_copies = []
    for k in range(1, n_dom):
        copy = pltpu.make_async_remote_copy(
            src_ref=wbuf.at[d],
            dst_ref=wbuf.at[d],
            send_sem=w_send.at[k],
            recv_sem=w_recv.at[k],
            device_id={"dom": lax.rem(d + k, n_dom)},
            device_id_type=MESH,
        )
        copy.start()
        w_copies.append(copy)

    low_d, high_d = d > 0, d < n_dom - 1
    low_s, high_s = s > 0, s < n_sub - 1
    down_d, up_d = {"dom": jnp.maximum(d - 1, 0)}, {"dom": jnp.minimum(d + 1, n_dom - 1)}
    down_s, up_s = {"sub": jnp.maximum(s - 1, 0)}, {"sub": jnp.minimum(s + 1, n_sub - 1)}

    def strip_copies(source, target, send, recv, devices):
        return [
            pltpu.make_async_remote_copy(
                src_ref=source.at[pl.ds(b * strip, strip)],
                dst_ref=target.at[pl.ds(b * strip, strip)],
                send_sem=send.at[b],
                recv_sem=recv.at[b],
                device_id=devices[b],
                device_id_type=MESH,
            )
            for b in range(4)
        ]

    def when_all(conditions, actions):
        for condition, action in zip(conditions, actions):
            pl.when(condition)(action)

    h_copies = strip_copies(strips, halo, h_send, h_recv, (down_d, up_d, down_s, up_s))
    h_to, h_from = (low_d, high_d, low_s, high_s), (high_d, low_d, high_s, low_s)
    when_all(h_to, [c.start for c in h_copies])

    for load in loads[6:9]:
        load.wait()
    count = count_ref[0]
    step = 256 if edges % 256 == 0 else LANES

    def indices(cut_e, at, carry):
        line = pl.ds(at // LANES, 1)
        dst = dst_ref[line, :]
        direction = dir_ref[line, :]
        row = jnp.floor((dst.astype(F32) + 0.5) * (1.0 / side)).astype(jnp.int32)
        col = dst - row * side
        src = jnp.where(
            direction == 0,
            jnp.where(row == side - 1, n_own + col, dst + side),
            jnp.where(
                direction == 1,
                jnp.where(row == 0, n_own + strip + col, dst - side),
                jnp.where(
                    direction == 2,
                    jnp.where(col == side - 1, n_own + 2 * strip + row, dst + 1),
                    jnp.where(col == 0, n_own + 3 * strip + row, dst - 1),
                ),
            ),
        )
        dst = jnp.where(iota((1, LANES), 1) + at < count, dst, -1)
        dst_cols = jnp.broadcast_to(dst, (LANES, LANES)).T
        src_cols = jnp.broadcast_to(src, (LANES, LANES)).T
        lane = iota((LANES, LANES), 1)
        for t in range((n_own + n_halo) // LANES):
            cut = slice(t * LANES, (t + 1) * LANES)
            s_src[cut_e, cut] = one_hot(src_cols == lane + t * LANES)
            if t < n_own // LANES:
                s_dst[cut_e, cut] = one_hot(dst_cols == lane + t * LANES)
        t_src[:, cut_e] = one_hot(iota((n_own + n_halo, LANES), 0) == src)
        t_dst[:, cut_e] = one_hot(iota((n_own, LANES), 0) == dst)
        return carry

    each_chunk(edges, LANES, indices)
    x_e[:, 0:lat] = feat_ref[...]

    def gather(cut, at, carry):
        x_e[cut, 2 * lat :] = mm(s_dst[cut, :], own[...]).astype(BF)
        x_e[cut, lat : 2 * lat] = mm(s_src[cut, 0:n_own], own[...]).astype(BF)
        return carry

    each_chunk(edges, step, gather)

    when_all(h_from, [c.wait_recv for c in h_copies])

    def gather_far(cut, at, carry):
        far = mm(s_src[cut, n_own:], halo[...])
        near = x_e[cut, lat : 2 * lat].astype(F32)
        x_e[cut, lat : 2 * lat] = (near + far).astype(BF)
        return carry

    each_chunk(edges, step, gather_far)
    for copy in w_copies:
        copy.wait_recv()

    def whole(name):
        at, size = off[name], rows[name]
        if size % 16 == 0:
            return jnp.concatenate([wbuf[n, at : at + size, :] for n in range(n_dom)], axis=0)
        padded = ceil_to(size, 16)
        parts = [wbuf[n, at : at + padded, :].astype(F32)[0:size, :] for n in range(n_dom)]
        return jnp.concatenate(parts, axis=0).astype(BF)

    w1e, w2e, w1n, w2n = whole("edge_in"), whole("edge_out"), whole("node_in"), whole("node_out")
    gains = sum(wbuf[n, off["gains"] : off["gains"] + 16, :].astype(F32) for n in range(n_dom))
    gain_edge, gain_node = gains[0:1, :], gains[1:2, :]

    def edge_forward(cut, at, carry):
        hidden = jnp.maximum(mm(x_e[cut, :], w1e), 0.0).astype(BF)
        hid_e[cut, :] = hidden
        normed, inv_std = layer_norm(mm(hidden, w2e))
        normed_e[cut, :] = normed
        inv_e[cut, :] = inv_std
        message = normed * gain_edge
        high = message.astype(BF)
        msg[cut, 0:lat] = high
        msg[cut, lat:] = (message - high.astype(F32)).astype(BF)
        return carry

    each_chunk(edges, step, edge_forward)
    both = mm(t_dst[...], msg[...])
    agg[...] = (both[:, 0:lat] + both[:, lat:]).astype(BF)

    for load in loads[9:]:
        load.wait()
    scale = (n_dom * n_sub * nodes) ** -0.5
    x_n[:, 0:lat] = own[...]
    x_n[:, lat:] = agg[...]

    def node_both(cut, at, gain_sum):
        inputs = x_n[cut, :]
        hidden = jnp.maximum(mm(inputs, w1n), 0.0).astype(BF)
        normed, inv_std = layer_norm(mm(hidden, w2n))
        upstream = ncot_ref[cut, :].astype(F32)
        graw = norm_back(upstream * gain_node, normed, inv_std).astype(BF)
        gpre = jnp.where(hidden > 0, mm_nt(graw, w2n), 0.0).astype(BF)
        hid_n[cut, :] = hidden
        graw_n[cut, :] = graw
        gpre_n[cut, :] = gpre
        grad_in = mm_nt(gpre, w1n)
        node_acc[cut, :] = upstream + grad_in[:, 0:lat]
        agg[cut, :] = grad_in[:, lat:].astype(BF)
        return gain_sum + jnp.sum(upstream * normed, axis=0, keepdims=True)

    node_step = max(n for n in range(16, 193, 16) if nodes % n == 0)
    node_gain = each_chunk(nodes, node_step, node_both, jnp.zeros((1, lat), F32))

    def pack(name, value):
        size = rows[name]
        for n in range(n_dom):
            g1[n, off[name] : off[name] + size, :] = (
                value[n * size : (n + 1) * size, :] * scale
            ).astype(BF)
            if size % 16:
                end = off[name] + ceil_to(size, 16)
                g1[n, off[name] + size : end, :] = jnp.zeros((end - off[name] - size, lat), BF)

    def dom_copies(first, last, send, recv):
        copies = []
        for k in range(1, n_dom):
            peer = lax.rem(d + k, n_dom)
            copy = pltpu.make_async_remote_copy(
                src_ref=g1.at[peer, pl.ds(first, last - first)],
                dst_ref=r1.at[k, pl.ds(first, last - first)],
                send_sem=send.at[k],
                recv_sem=recv.at[k],
                device_id={"dom": peer},
                device_id_type=MESH,
            )
            copy.start()
            copies.append(copy)
        return copies

    pack("node_in", mm_tn(x_n[0:nodes, :], gpre_n[...]))
    pack("node_out", mm_tn(hid_n[...], graw_n[...]))
    n_copies = dom_copies(0, plan.node_part, n_send, n_recv)

    def edge_backward(cut, at, gain_sum):
        cot = ecot_ref[cut, :].astype(F32)
        live = iota((step, lat), 0) + at < count
        upstream = jnp.where(live, cot, 0.0) + mm(s_dst[cut, :], agg[...])
        normed, inv_std = normed_e[cut, :], inv_e[cut, :]
        graw = norm_back(upstream * gain_edge, normed, inv_std).astype(BF)
        graw_e[cut, :] = graw
        gpre_e[cut, :] = jnp.where(hid_e[cut, :] > 0, mm_nt(graw, w2e), 0.0).astype(BF)
        return gain_sum + jnp.sum(upstream * normed, axis=0, keepdims=True)

    edge_gain = each_chunk(edges, step, edge_backward, jnp.zeros((1, lat), F32))

    pack("edge_in", mm_tn(x_e[...], gpre_e[...]))
    pack("edge_out", mm_tn(hid_e[...], graw_e[...]))
    row16 = iota((16, lat), 0)
    gains16 = jnp.where(row16 == 0, edge_gain, jnp.where(row16 == 1, node_gain, 0.0))
    for n in range(n_dom):
        g1[n, off["gains"] : off["gains"] + 16, :] = (gains16 * scale).astype(BF)
        if plan.total > plan.shard:
            g1[n, plan.shard :, :] = jnp.zeros((plan.total - plan.shard, lat), BF)
    e_copies = dom_copies(plan.node_part, plan.total, e_send, e_recv)

    w_src, w_dst = w1e[lat : 2 * lat, :], w1e[2 * lat :, :]
    back = mm(t_src[n_own:, :], gpre_e[...]).astype(BF)
    gstrips[...] = mm_nt(back, w_src).astype(BF)
    b_copies = strip_copies(gstrips, ghalo, b_send, b_recv, (up_d, down_d, up_s, down_s))
    when_all(h_from, [c.start for c in b_copies])


    def edge_result(cut, at, carry):
        grad = mm_nt(gpre_e[cut, :], w1e[0:lat, :])
        edge_out[cut, :] = (ecot_ref[cut, :].astype(F32) + grad).astype(BF)
        return carry

    each_chunk(edges, step, edge_result)
    stores[1].start()

    at_src = mm(t_src[0:n_own, :], gpre_e[...]).astype(BF)
    at_dst = mm(t_dst[...], gpre_e[...]).astype(BF)
    spread = mm_nt(at_src, w_src) + mm_nt(at_dst, w_dst)

    for copy in n_copies + e_copies:
        copy.wait_recv()
    acc = g1[d].astype(F32)
    for k in range(1, n_dom):
        acc = acc + r1[k].astype(F32)
    p2[...] = acc.astype(BF).reshape(n_sub, plan.piece, lat)
    q_copies = []
    for k in range(1, n_sub):
        peer = lax.rem(s + k, n_sub)
        copy = pltpu.make_async_remote_copy(
            src_ref=p2.at[peer],
            dst_ref=r2.at[k],
            send_sem=q_send.at[k],
            recv_sem=q_recv.at[k],
            device_id={"sub": peer},
            device_id_type=MESH,
        )
        copy.start()
        q_copies.append(copy)

    when_all(h_to, [c.wait_recv for c in b_copies])
    pos = iota((n_own, n_halo), 1)
    node_id = iota((n_own, n_halo), 0)
    picked = jnp.zeros((n_own, n_halo), jnp.bool_)
    for b in range(4):
        at = pos - b * strip
        border = (at, (side - 1) * side + at, at * side, at * side + side - 1)[b]
        picked = picked | ((at >= 0) & (at < side) & (node_id == border))
    spread = spread + mm(one_hot(picked), ghalo[...])
    node_out[...] = (node_acc[...] + spread[0:nodes, :]).astype(BF)
    stores[0].start()

    for copy in q_copies:
        copy.wait_recv()
    acc = p2[s].astype(F32)
    for k in range(1, n_sub):
        acc = acc + r2[k].astype(F32)
    fin[s] = acc.astype(BF)
    f_copies = []
    for k in range(1, n_sub):
        copy = pltpu.make_async_remote_copy(
            src_ref=fin.at[s],
            dst_ref=fin.at[s],
            send_sem=f_send.at[k],
            recv_sem=f_recv.at[k],
            device_id={"sub": lax.rem(s + k, n_sub)},
            device_id_type=MESH,
        )
        copy.start()
        f_copies.append(copy)
    for copy in f_copies:
        copy.wait_recv()
    result = fin[...].reshape(plan.total, lat)
    for name, ref in (
        ("edge_in", gei_out),
        ("edge_out", geo_out),
        ("node_in", gni_out),
        ("node_out", gno_out),
    ):
        ref[...] = result[off[name] : off[name] + ceil_to(rows[name], 16), :].astype(F32)[
            0 : rows[name], :
        ]
    gain_out[...] = mm_nt(result[off["gains"] : off["gains"] + 16, :], place)[0:2, :]
    for store in stores[2:]:
        store.start()

    for copy in w_copies + n_copies + e_copies + q_copies + f_copies:
        copy.wait_send()
    when_all(h_to, [c.wait_send for c in h_copies])
    when_all(h_from, [c.wait_send for c in b_copies])
    for store in stores:
        store.wait()


def write_out(*refs):
    sources, targets, stage, in_sem, out_sem = refs[:7], refs[7:14], refs[14:21], *refs[21:]
    reads = [pltpu.make_async_copy(sources[i], stage[i], in_sem.at[i]) for i in range(7)]
    writes = [pltpu.make_async_copy(stage[i], targets[i], out_sem.at[i]) for i in range(7)]
    for read in reads:
        read.start()
    for read, write in zip(reads, writes):
        read.wait()
        write.start()
    for write in writes:
        write.wait()


def shards(
    node_feat,
    edge_feat,
    edge_dst,
    edge_dir,
    edge_count,
    w_edge_in,
    w_edge_out,
    w_node_in,
    w_node_out,
    gains,
    node_cot,
    edge_cot,
):
    n_dom, n_sub = lax.axis_size("dom"), lax.axis_size("sub")
    side, _, lat = node_feat.shape
    edges = edge_feat.shape[0]
    rows = {
        "edge_in": w_edge_in.shape[0],
        "edge_out": w_edge_out.shape[0],
        "node_in": w_node_in.shape[0],
        "node_out": w_node_out.shape[0],
    }
    plan = Plan(n_dom, n_sub, side, edges, lat, rows)
    nodes, n_own, n_halo = plan.nodes, plan.own, plan.halo
    table = n_own + n_halo
    dma = pltpu.SemaphoreType.DMA
    hbm = pl.BlockSpec(memory_space=pltpu.HBM)
    vmem_limit = 64 * 1024 * 1024
    out_shape = [
        jax.ShapeDtypeStruct((nodes, lat), BF),
        jax.ShapeDtypeStruct((edges, lat), BF),
        jax.ShapeDtypeStruct(w_edge_in.shape, F32),
        jax.ShapeDtypeStruct(w_edge_out.shape, F32),
        jax.ShapeDtypeStruct(w_node_in.shape, F32),
        jax.ShapeDtypeStruct(w_node_out.shape, F32),
        jax.ShapeDtypeStruct(gains.shape, F32),
    ]
    outs = pl.pallas_call(
        functools.partial(kernel, plan),
        out_shape=out_shape,
        in_specs=[hbm] * 4 + [pl.BlockSpec(memory_space=pltpu.SMEM)] + [hbm] * 7,
        out_specs=[hbm] * 7,
        scratch_shapes=[pltpu.VMEM(out.shape, out.dtype) for out in out_shape]
        + [
            dma((7,)),
            pltpu.VMEM((nodes, lat), BF),
            pltpu.VMEM((edges, lat), BF),
            pltpu.VMEM((edges // LANES, LANES), jnp.int32),
            pltpu.VMEM((edges // LANES, LANES), jnp.int32),
            pltpu.VMEM(w_edge_in.shape, BF),
            pltpu.VMEM(w_edge_out.shape, BF),
            pltpu.VMEM(w_node_in.shape, BF),
            pltpu.VMEM(w_node_out.shape, BF),
            pltpu.VMEM(gains.shape, BF),
            pltpu.VMEM((nodes, lat), BF),
            pltpu.VMEM((edges, lat), BF),
            dma((11,)),
            pltpu.VMEM((n_dom, plan.shard, lat), BF),
            pltpu.VMEM((n_own, lat), BF),
            pltpu.VMEM((n_halo, lat), BF),
            pltpu.VMEM((n_halo, lat), BF),
            pltpu.VMEM((n_halo, lat), BF),
            pltpu.VMEM((n_halo, lat), BF),
            pltpu.VMEM((edges, n_own), BF),
            pltpu.VMEM((edges, table), BF),
            pltpu.VMEM((n_own, edges), BF),
            pltpu.VMEM((table, edges), BF),
            pltpu.VMEM((edges, 3 * lat), BF),
            pltpu.VMEM((edges, lat), BF),
            pltpu.VMEM((edges, lat), F32),
            pltpu.VMEM((edges, 1), F32),
            pltpu.VMEM((edges, lat), BF),
            pltpu.VMEM((edges, lat), BF),
            pltpu.VMEM((edges, 2 * lat), BF),
            pltpu.VMEM((n_own, lat), BF),
            pltpu.VMEM((n_own, 2 * lat), BF),
            pltpu.VMEM((nodes, lat), BF),
            pltpu.VMEM((nodes, lat), BF),
            pltpu.VMEM((nodes, lat), BF),
            pltpu.VMEM((nodes, lat), F32),
            pltpu.VMEM((n_dom, plan.total, lat), BF),
            pltpu.VMEM((n_dom, plan.total, lat), BF),
            pltpu.VMEM((n_sub, plan.piece, lat), BF),
            pltpu.VMEM((n_sub, plan.piece, lat), BF),
            pltpu.VMEM((n_sub, plan.piece, lat), BF),
            dma((n_dom,)),
            dma((n_dom,)),
            dma((4,)),
            dma((4,)),
            dma((4,)),
            dma((4,)),
            dma((n_dom,)),
            dma((n_dom,)),
            dma((n_dom,)),
            dma((n_dom,)),
            dma((n_sub,)),
            dma((n_sub,)),
            dma((n_sub,)),
            dma((n_sub,)),
        ],
        compiler_params=pltpu.CompilerParams(
            collective_id=0, has_side_effects=True, vmem_limit_bytes=vmem_limit
        ),
        name="graph_layer_backward",
    )(
        node_feat.reshape(nodes, lat),
        edge_feat,
        edge_dst.reshape(edges // LANES, LANES),
        edge_dir.reshape(edges // LANES, LANES),
        edge_count,
        w_edge_in,
        w_edge_out,
        w_node_in,
        w_node_out,
        gains,
        node_cot.reshape(nodes, lat),
        edge_cot,
    )
    outs = pl.pallas_call(
        write_out,
        out_shape=out_shape,
        in_specs=[hbm] * 7,
        out_specs=[hbm] * 7,
        scratch_shapes=[pltpu.VMEM(out.shape, out.dtype) for out in out_shape]
        + [dma((7,)), dma((7,))],
        compiler_params=pltpu.CompilerParams(vmem_limit_bytes=vmem_limit),
        name="write_results",
    )(*outs)
    return (outs[0].reshape(node_feat.shape), *outs[1:])


def solution(mesh):
    in_specs = (
        P("dom", "sub", None),
        P(("dom", "sub"), None),
        P(("dom", "sub")),
        P(("dom", "sub")),
        P(("dom", "sub")),
        P("dom", None),
        P("dom", None),
        P("dom", None),
        P("dom", None),
        P(None, "dom"),
        P("dom", "sub", None),
        P(("dom", "sub"), None),
    )
    out_specs = (
        P("dom", "sub", None),
        P(("dom", "sub"), None),
        P("dom", None),
        P("dom", None),
        P("dom", None),
        P("dom", None),
        P(None, "dom"),
    )
    return jax.shard_map(shards, mesh=mesh, in_specs=in_specs, out_specs=out_specs, check_vma=False)
```

```python
import functools

import jax
import jax.numpy as jnp
from jax import lax
from jax.experimental import pallas as pl
from jax.experimental.pallas import tpu as pltpu
from jax.sharding import PartitionSpec as P

MESH = pl.DeviceIdType.MESH
BF = jnp.bfloat16
F32 = jnp.float32
LANES = 128


def ceil_to(value, step):
    return -(-value // step) * step


def mm(a, b):
    return jnp.dot(a, b, preferred_element_type=F32)


def mm_nt(a, b):
    return lax.dot_general(a, b, (((1,), (1,)), ((), ())), preferred_element_type=F32)


def mm_tn(a, b):
    return lax.dot_general(a, b, (((0,), (0,)), ((), ())), preferred_element_type=F32)


def iota(shape, dim):
    return lax.broadcasted_iota(jnp.int32, shape, dim)


def one_hot(mask):
    return jnp.where(mask, 1.0, 0.0).astype(BF)


def layer_norm(raw_out):
    average = jnp.mean(raw_out, axis=-1, keepdims=True)
    centered = raw_out - average
    inv_std = lax.rsqrt(jnp.mean(centered * centered, axis=-1, keepdims=True) + 1e-05)
    return centered * inv_std, inv_std


def norm_back(upstream, normed, inv_std):
    return (
        upstream
        - jnp.mean(upstream, axis=-1, keepdims=True)
        - normed * jnp.mean(upstream * normed, axis=-1, keepdims=True)
    ) * inv_std


def each_chunk(total, step, body, init=0):
    carry = init
    for at in range(0, total, step):
        carry = body(slice(at, at + step), at, carry)
    return carry


class Plan:
    def __init__(self, n_dom, n_sub, side, edges, latent, rows):
        self.n_dom, self.n_sub = n_dom, n_sub
        self.side, self.edges, self.latent = side, edges, latent
        self.nodes = side * side
        self.own = ceil_to(self.nodes, LANES)
        self.strip = ceil_to(side, 16)
        self.halo = ceil_to(4 * self.strip, LANES)
        self.rows = rows
        at = 0
        self.off = {}
        for name in ("node_in", "node_out", "edge_in", "edge_out", "gains"):
            self.off[name] = at
            at += 16 if name == "gains" else ceil_to(rows[name], 16)
        self.shard = at
        self.node_part = self.off["edge_in"]
        self.piece = ceil_to(-(-at // n_sub), 16)
        self.total = self.piece * n_sub


def kernel(
    plan,
    node_hbm,
    feat_hbm,
    dst_hbm,
    dir_hbm,
    count_ref,
    wei_hbm,
    weo_hbm,
    wni_hbm,
    wno_hbm,
    gains_hbm,
    ncot_hbm,
    ecot_hbm,
    node_out_hbm,
    edge_out_hbm,
    gei_out_hbm,
    geo_out_hbm,
    gni_out_hbm,
    gno_out_hbm,
    gain_out_hbm,
    node_out,
    edge_out,
    gei_out,
    geo_out,
    gni_out,
    gno_out,
    gain_out,
    out_sem,
    node_ref,
    feat_ref,
    dst_ref,
    dir_ref,
    wei_ref,
    weo_ref,
    wni_ref,
    wno_ref,
    gains_ref,
    ncot_ref,
    ecot_ref,
    in_sem,
    wbuf,
    table,
    strips,
    gstrips,
    ghalo,
    s_dst,
    s_src,
    t_dst,
    t_src,
    x_e,
    hid_e,
    normed_e,
    inv_e,
    gpre_e,
    graw_e,
    msg,
    agg,
    x_n,
    hid_n,
    graw_n,
    gpre_n,
    node_acc,
    g1,
    r1,
    p2,
    r2,
    fin,
    w_send,
    w_recv,
    h_send,
    h_recv,
    b_send,
    b_recv,
    n_send,
    n_recv,
    e_send,
    e_recv,
    q_send,
    q_recv,
    f_send,
    f_recv,
):
    n_dom, n_sub, side, edges = plan.n_dom, plan.n_sub, plan.side, plan.edges
    nodes, n_own, strip, lat = plan.nodes, plan.own, plan.strip, plan.latent
    n_halo, off, rows = plan.halo, plan.off, plan.rows
    d = lax.axis_index("dom")
    s = lax.axis_index("sub")

    pairs = (
        (wei_hbm, wei_ref),
        (weo_hbm, weo_ref),
        (wni_hbm, wni_ref),
        (wno_hbm, wno_ref),
        (gains_hbm, gains_ref),
        (node_hbm, node_ref),
        (dst_hbm, dst_ref),
        (dir_hbm, dir_ref),
        (feat_hbm, feat_ref),
        (ncot_hbm, ncot_ref),
        (ecot_hbm, ecot_ref),
    )
    loads = [
        pltpu.make_async_copy(hbm, ref, in_sem.at[i]) for i, (hbm, ref) in enumerate(pairs)
    ]
    for load in loads:
        load.start()
    pairs = (
        (node_out, node_out_hbm),
        (edge_out, edge_out_hbm),
        (gei_out, gei_out_hbm),
        (geo_out, geo_out_hbm),
        (gni_out, gni_out_hbm),
        (gno_out, gno_out_hbm),
        (gain_out, gain_out_hbm),
    )
    stores = [
        pltpu.make_async_copy(ref, hbm, out_sem.at[i]) for i, (ref, hbm) in enumerate(pairs)
    ]

    table[n_own:, :] = jnp.zeros((n_halo, lat), BF)
    ghalo[...] = jnp.zeros_like(ghalo)
    barrier = pltpu.get_barrier_semaphore()
    for k in range(1, n_dom):
        pl.semaphore_signal(
            barrier, inc=1, device_id={"dom": lax.rem(d + k, n_dom)}, device_id_type=MESH
        )
    for k in range(1, n_sub):
        pl.semaphore_signal(
            barrier, inc=1, device_id={"sub": lax.rem(s + k, n_sub)}, device_id_type=MESH
        )

    for load in loads[:5]:
        load.wait()
    shard_refs = {"edge_in": wei_ref, "edge_out": weo_ref, "node_in": wni_ref, "node_out": wno_ref}
    for name, ref in shard_refs.items():
        wbuf[d, off[name] : off[name] + rows[name], :] = ref[...]
    width = gains_ref.shape[1]
    gains32 = gains_ref[...].astype(F32)
    row16 = iota((16, width), 0)
    gains16 = jnp.where(
        row16 == 0, gains32[0:1, :], jnp.where(row16 == 1, gains32[1:2, :], 0.0)
    ).astype(BF)
    place = one_hot(iota((width, lat), 1) == iota((width, lat), 0) + d * width)
    wbuf[d, off["gains"] : off["gains"] + 16, :] = mm(gains16, place).astype(BF)

    loads[5].wait()
    table[0:nodes, :] = node_ref[...]
    table[nodes:n_own, :] = jnp.zeros((n_own - nodes, lat), BF)
    pos = iota((strip, n_own), 0)
    node_id = iota((strip, n_own), 1)
    inside = pos < side
    borders = (pos, (side - 1) * side + pos, pos * side, pos * side + side - 1)
    for b in range(4):
        select = one_hot((node_id == borders[b]) & inside)
        strips[b * strip : (b + 1) * strip, :] = mm(select, table[0:n_own, :]).astype(BF)

    pl.semaphore_wait(barrier, (n_dom - 1) + (n_sub - 1))

    w_copies = []
    for k in range(1, n_dom):
        copy = pltpu.make_async_remote_copy(
            src_ref=wbuf.at[d],
            dst_ref=wbuf.at[d],
            send_sem=w_send.at[k],
            recv_sem=w_recv.at[k],
            device_id={"dom": lax.rem(d + k, n_dom)},
            device_id_type=MESH,
        )
        copy.start()
        w_copies.append(copy)

    low_d, high_d = d > 0, d < n_dom - 1
    low_s, high_s = s > 0, s < n_sub - 1
    down_d, up_d = {"dom": jnp.maximum(d - 1, 0)}, {"dom": jnp.minimum(d + 1, n_dom - 1)}
    down_s, up_s = {"sub": jnp.maximum(s - 1, 0)}, {"sub": jnp.minimum(s + 1, n_sub - 1)}

    def strip_copies(source, target, first, send, recv, devices):
        return [
            pltpu.make_async_remote_copy(
                src_ref=source.at[pl.ds(b * strip, strip)],
                dst_ref=target.at[pl.ds(first + b * strip, strip)],
                send_sem=send.at[b],
                recv_sem=recv.at[b],
                device_id=devices[b],
                device_id_type=MESH,
            )
            for b in range(4)
        ]

    def when_all(conditions, actions):
        for condition, action in zip(conditions, actions):
            pl.when(condition)(action)

    h_copies = strip_copies(strips, table, n_own, h_send, h_recv, (down_d, up_d, down_s, up_s))
    h_to, h_from = (low_d, high_d, low_s, high_s), (high_d, low_d, high_s, low_s)
    when_all(h_to, [c.start for c in h_copies])

    for load in loads[6:9]:
        load.wait()
    count = count_ref[0]
    step = 256 if edges % 256 == 0 else LANES

    def indices(cut_e, at, carry):
        line = slice(at // LANES, at // LANES + 1)
        dst = dst_ref[line, :]
        direction = dir_ref[line, :]
        row = jnp.floor((dst.astype(F32) + 0.5) * (1.0 / side)).astype(jnp.int32)
        col = dst - row * side
        src = jnp.where(
            direction == 0,
            jnp.where(row == side - 1, n_own + col, dst + side),
            jnp.where(
                direction == 1,
                jnp.where(row == 0, n_own + strip + col, dst - side),
                jnp.where(
                    direction == 2,
                    jnp.where(col == side - 1, n_own + 2 * strip + row, dst + 1),
                    jnp.where(col == 0, n_own + 3 * strip + row, dst - 1),
                ),
            ),
        )
        dst = jnp.where(iota((1, LANES), 1) + at < count, dst, -1)
        dst_cols = jnp.broadcast_to(dst, (LANES, LANES)).T
        src_cols = jnp.broadcast_to(src, (LANES, LANES)).T
        lane = iota((LANES, LANES), 1)
        for t in range((n_own + n_halo) // LANES):
            cut = slice(t * LANES, (t + 1) * LANES)
            s_src[cut_e, cut] = one_hot(src_cols == lane + t * LANES)
            if t < n_own // LANES:
                s_dst[cut_e, cut] = one_hot(dst_cols == lane + t * LANES)
        t_src[:, cut_e] = one_hot(iota((n_own + n_halo, LANES), 0) == src)
        t_dst[:, cut_e] = one_hot(iota((n_own, LANES), 0) == dst)
        return carry

    each_chunk(edges, LANES, indices)
    x_e[:, 0:lat] = feat_ref[...]

    def gather_dst(cut, at, carry):
        x_e[cut, 2 * lat :] = mm(s_dst[cut, :], table[0:n_own, :]).astype(BF)
        return carry

    each_chunk(edges, step, gather_dst)
    when_all(h_from, [c.wait_recv for c in h_copies])

    def gather_src(cut, at, carry):
        x_e[cut, lat : 2 * lat] = mm(s_src[cut, :], table[...]).astype(BF)
        return carry

    each_chunk(edges, step, gather_src)
    for copy in w_copies:
        copy.wait_recv()

    def whole(name):
        at, size = off[name], rows[name]
        if size % 16 == 0:
            return jnp.concatenate([wbuf[n, at : at + size, :] for n in range(n_dom)], axis=0)
        padded = ceil_to(size, 16)
        parts = [wbuf[n, at : at + padded, :].astype(F32)[0:size, :] for n in range(n_dom)]
        return jnp.concatenate(parts, axis=0).astype(BF)

    w1e, w2e, w1n, w2n = whole("edge_in"), whole("edge_out"), whole("node_in"), whole("node_out")
    gains = sum(wbuf[n, off["gains"] : off["gains"] + 16, :].astype(F32) for n in range(n_dom))
    gain_edge, gain_node = gains[0:1, :], gains[1:2, :]

    def edge_forward(cut, at, carry):
        hidden = jnp.maximum(mm(x_e[cut, :], w1e), 0.0).astype(BF)
        hid_e[cut, :] = hidden
        normed, inv_std = layer_norm(mm(hidden, w2e))
        normed_e[cut, :] = normed
        inv_e[cut, :] = inv_std
        message = normed * gain_edge
        high = message.astype(BF)
        msg[cut, 0:lat] = high
        msg[cut, lat:] = (message - high.astype(F32)).astype(BF)
        return carry

    each_chunk(edges, step, edge_forward)
    both = mm(t_dst[...], msg[...])
    agg[...] = (both[:, 0:lat] + both[:, lat:]).astype(BF)

    for load in loads[9:]:
        load.wait()
    scale = (n_dom * n_sub * nodes) ** -0.5
    x_n[:, 0:lat] = table[0:n_own, :]
    x_n[:, lat:] = agg[...]

    def node_both(cut, at, gain_sum):
        inputs = x_n[cut, :]
        hidden = jnp.maximum(mm(inputs, w1n), 0.0).astype(BF)
        normed, inv_std = layer_norm(mm(hidden, w2n))
        upstream = ncot_ref[cut, :].astype(F32)
        graw = norm_back(upstream * gain_node, normed, inv_std).astype(BF)
        gpre = jnp.where(hidden > 0, mm_nt(graw, w2n), 0.0).astype(BF)
        hid_n[cut, :] = hidden
        graw_n[cut, :] = graw
        gpre_n[cut, :] = gpre
        grad_in = mm_nt(gpre, w1n)
        node_acc[cut, :] = upstream + grad_in[:, 0:lat]
        agg[cut, :] = grad_in[:, lat:].astype(BF)
        return gain_sum + jnp.sum(upstream * normed, axis=0, keepdims=True)

    node_step = max(n for n in range(16, 193, 16) if nodes % n == 0)
    node_gain = each_chunk(nodes, node_step, node_both, jnp.zeros((1, lat), F32))

    def pack(name, value):
        size = rows[name]
        for n in range(n_dom):
            g1[n, off[name] : off[name] + size, :] = (
                value[n * size : (n + 1) * size, :] * scale
            ).astype(BF)
            if size % 16:
                end = off[name] + ceil_to(size, 16)
                g1[n, off[name] + size : end, :] = jnp.zeros((end - off[name] - size, lat), BF)

    def dom_copies(first, last, send, recv):
        copies = []
        for k in range(1, n_dom):
            peer = lax.rem(d + k, n_dom)
            copy = pltpu.make_async_remote_copy(
                src_ref=g1.at[peer, pl.ds(first, last - first)],
                dst_ref=r1.at[k, pl.ds(first, last - first)],
                send_sem=send.at[k],
                recv_sem=recv.at[k],
                device_id={"dom": peer},
                device_id_type=MESH,
            )
            copy.start()
            copies.append(copy)
        return copies

    pack("node_in", mm_tn(gpre_n[...], x_n[0:nodes, :]).T)
    pack("node_out", mm_tn(hid_n[...], graw_n[...]))
    n_copies = dom_copies(0, plan.node_part, n_send, n_recv)

    def edge_backward(cut, at, gain_sum):
        cot = ecot_ref[cut, :].astype(F32)
        live = iota((step, lat), 0) + at < count
        upstream = jnp.where(live, cot, 0.0) + mm(s_dst[cut, :], agg[...])
        normed, inv_std = normed_e[cut, :], inv_e[cut, :]
        graw = norm_back(upstream * gain_edge, normed, inv_std).astype(BF)
        graw_e[cut, :] = graw
        gpre_e[cut, :] = jnp.where(hid_e[cut, :] > 0, mm_nt(graw, w2e), 0.0).astype(BF)
        return gain_sum + jnp.sum(upstream * normed, axis=0, keepdims=True)

    edge_gain = each_chunk(edges, step, edge_backward, jnp.zeros((1, lat), F32))

    pack("edge_in", mm_tn(gpre_e[...], x_e[...]).T)
    pack("edge_out", mm_tn(hid_e[...], graw_e[...]))
    row16 = iota((16, lat), 0)
    gains16 = jnp.where(row16 == 0, edge_gain, jnp.where(row16 == 1, node_gain, 0.0))
    for n in range(n_dom):
        g1[n, off["gains"] : off["gains"] + 16, :] = (gains16 * scale).astype(BF)
        if plan.total > plan.shard:
            g1[n, plan.shard :, :] = jnp.zeros((plan.total - plan.shard, lat), BF)
    e_copies = dom_copies(plan.node_part, plan.total, e_send, e_recv)

    w_src, w_dst = w1e[lat : 2 * lat, :], w1e[2 * lat :, :]
    back = mm(t_src[n_own:, :], gpre_e[...]).astype(BF)
    gstrips[...] = mm_nt(back, w_src).astype(BF)
    b_copies = strip_copies(gstrips, ghalo, 0, b_send, b_recv, (up_d, down_d, up_s, down_s))
    when_all(h_from, [c.start for c in b_copies])


    def edge_result(cut, at, carry):
        grad = mm_nt(gpre_e[cut, :], w1e[0:lat, :])
        edge_out[cut, :] = (ecot_ref[cut, :].astype(F32) + grad).astype(BF)
        return carry

    each_chunk(edges, step, edge_result)
    stores[1].start()

    at_src = mm(t_src[0:n_own, :], gpre_e[...]).astype(BF)
    at_dst = mm(t_dst[...], gpre_e[...]).astype(BF)
    spread = mm_nt(at_src, w_src) + mm_nt(at_dst, w_dst)

    for copy in n_copies + e_copies:
        copy.wait_recv()
    acc = g1[d].astype(F32)
    for k in range(1, n_dom):
        acc = acc + r1[k].astype(F32)
    p2[...] = acc.astype(BF).reshape(n_sub, plan.piece, lat)
    q_copies = []
    for k in range(1, n_sub):
        peer = lax.rem(s + k, n_sub)
        copy = pltpu.make_async_remote_copy(
            src_ref=p2.at[peer],
            dst_ref=r2.at[k],
            send_sem=q_send.at[k],
            recv_sem=q_recv.at[k],
            device_id={"sub": peer},
            device_id_type=MESH,
        )
        copy.start()
        q_copies.append(copy)

    when_all(h_to, [c.wait_recv for c in b_copies])
    pos = iota((n_own, n_halo), 1)
    node_id = iota((n_own, n_halo), 0)
    picked = jnp.zeros((n_own, n_halo), jnp.bool_)
    for b in range(4):
        at = pos - b * strip
        border = (at, (side - 1) * side + at, at * side, at * side + side - 1)[b]
        picked = picked | ((at >= 0) & (at < side) & (node_id == border))
    spread = spread + mm(one_hot(picked), ghalo[...])
    node_out[...] = (node_acc[...] + spread[0:nodes, :]).astype(BF)
    stores[0].start()

    for copy in q_copies:
        copy.wait_recv()
    acc = p2[s].astype(F32)
    for k in range(1, n_sub):
        acc = acc + r2[k].astype(F32)
    fin[s] = acc.astype(BF)
    f_copies = []
    for k in range(1, n_sub):
        copy = pltpu.make_async_remote_copy(
            src_ref=fin.at[s],
            dst_ref=fin.at[s],
            send_sem=f_send.at[k],
            recv_sem=f_recv.at[k],
            device_id={"sub": lax.rem(s + k, n_sub)},
            device_id_type=MESH,
        )
        copy.start()
        f_copies.append(copy)
    for copy in f_copies:
        copy.wait_recv()
    result = fin[...].reshape(plan.total, lat)
    for name, ref in (
        ("edge_in", gei_out),
        ("edge_out", geo_out),
        ("node_in", gni_out),
        ("node_out", gno_out),
    ):
        ref[...] = result[off[name] : off[name] + ceil_to(rows[name], 16), :].astype(F32)[
            0 : rows[name], :
        ]
    gain_out[...] = mm_nt(result[off["gains"] : off["gains"] + 16, :], place)[0:2, :]
    for store in stores[2:]:
        store.start()

    for copy in w_copies + n_copies + e_copies + q_copies + f_copies:
        copy.wait_send()
    when_all(h_to, [c.wait_send for c in h_copies])
    when_all(h_from, [c.wait_send for c in b_copies])
    for store in stores:
        store.wait()


def write_out(*refs):
    sources, targets, stage, in_sem, out_sem = refs[:7], refs[7:14], refs[14:21], *refs[21:]
    reads = [pltpu.make_async_copy(sources[i], stage[i], in_sem.at[i]) for i in range(7)]
    writes = [pltpu.make_async_copy(stage[i], targets[i], out_sem.at[i]) for i in range(7)]
    for read in reads:
        read.start()
    for read, write in zip(reads, writes):
        read.wait()
        write.start()
    for write in writes:
        write.wait()


def shards(
    node_feat,
    edge_feat,
    edge_dst,
    edge_dir,
    edge_count,
    w_edge_in,
    w_edge_out,
    w_node_in,
    w_node_out,
    gains,
    node_cot,
    edge_cot,
):
    n_dom, n_sub = lax.axis_size("dom"), lax.axis_size("sub")
    side, _, lat = node_feat.shape
    edges = edge_feat.shape[0]
    rows = {
        "edge_in": w_edge_in.shape[0],
        "edge_out": w_edge_out.shape[0],
        "node_in": w_node_in.shape[0],
        "node_out": w_node_out.shape[0],
    }
    plan = Plan(n_dom, n_sub, side, edges, lat, rows)
    nodes, n_own, n_halo = plan.nodes, plan.own, plan.halo
    table = n_own + n_halo
    dma = pltpu.SemaphoreType.DMA
    hbm = pl.BlockSpec(memory_space=pltpu.HBM)
    vmem_limit = 64 * 1024 * 1024
    out_shape = [
        jax.ShapeDtypeStruct((nodes, lat), BF),
        jax.ShapeDtypeStruct((edges, lat), BF),
        jax.ShapeDtypeStruct(w_edge_in.shape, F32),
        jax.ShapeDtypeStruct(w_edge_out.shape, F32),
        jax.ShapeDtypeStruct(w_node_in.shape, F32),
        jax.ShapeDtypeStruct(w_node_out.shape, F32),
        jax.ShapeDtypeStruct(gains.shape, F32),
    ]
    outs = pl.pallas_call(
        functools.partial(kernel, plan),
        out_shape=out_shape,
        in_specs=[hbm] * 4 + [pl.BlockSpec(memory_space=pltpu.SMEM)] + [hbm] * 7,
        out_specs=[hbm] * 7,
        scratch_shapes=[pltpu.VMEM(out.shape, out.dtype) for out in out_shape]
        + [
            dma((7,)),
            pltpu.VMEM((nodes, lat), BF),
            pltpu.VMEM((edges, lat), BF),
            pltpu.VMEM((edges // LANES, LANES), jnp.int32),
            pltpu.VMEM((edges // LANES, LANES), jnp.int32),
            pltpu.VMEM(w_edge_in.shape, BF),
            pltpu.VMEM(w_edge_out.shape, BF),
            pltpu.VMEM(w_node_in.shape, BF),
            pltpu.VMEM(w_node_out.shape, BF),
            pltpu.VMEM(gains.shape, BF),
            pltpu.VMEM((nodes, lat), BF),
            pltpu.VMEM((edges, lat), BF),
            dma((11,)),
            pltpu.VMEM((n_dom, plan.shard, lat), BF),
            pltpu.VMEM((table, lat), BF),
            pltpu.VMEM((n_halo, lat), BF),
            pltpu.VMEM((n_halo, lat), BF),
            pltpu.VMEM((n_halo, lat), BF),
            pltpu.VMEM((edges, n_own), BF),
            pltpu.VMEM((edges, table), BF),
            pltpu.VMEM((n_own, edges), BF),
            pltpu.VMEM((table, edges), BF),
            pltpu.VMEM((edges, 3 * lat), BF),
            pltpu.VMEM((edges, lat), BF),
            pltpu.VMEM((edges, lat), F32),
            pltpu.VMEM((edges, 1), F32),
            pltpu.VMEM((edges, lat), BF),
            pltpu.VMEM((edges, lat), BF),
            pltpu.VMEM((edges, 2 * lat), BF),
            pltpu.VMEM((n_own, lat), BF),
            pltpu.VMEM((n_own, 2 * lat), BF),
            pltpu.VMEM((nodes, lat), BF),
            pltpu.VMEM((nodes, lat), BF),
            pltpu.VMEM((nodes, lat), BF),
            pltpu.VMEM((nodes, lat), F32),
            pltpu.VMEM((n_dom, plan.total, lat), BF),
            pltpu.VMEM((n_dom, plan.total, lat), BF),
            pltpu.VMEM((n_sub, plan.piece, lat), BF),
            pltpu.VMEM((n_sub, plan.piece, lat), BF),
            pltpu.VMEM((n_sub, plan.piece, lat), BF),
            dma((n_dom,)),
            dma((n_dom,)),
            dma((4,)),
            dma((4,)),
            dma((4,)),
            dma((4,)),
            dma((n_dom,)),
            dma((n_dom,)),
            dma((n_dom,)),
            dma((n_dom,)),
            dma((n_sub,)),
            dma((n_sub,)),
            dma((n_sub,)),
            dma((n_sub,)),
        ],
        compiler_params=pltpu.CompilerParams(
            collective_id=0, has_side_effects=True, vmem_limit_bytes=vmem_limit
        ),
        name="graph_layer_backward",
    )(
        node_feat.reshape(nodes, lat),
        edge_feat,
        edge_dst.reshape(edges // LANES, LANES),
        edge_dir.reshape(edges // LANES, LANES),
        edge_count,
        w_edge_in,
        w_edge_out,
        w_node_in,
        w_node_out,
        gains,
        node_cot.reshape(nodes, lat),
        edge_cot,
    )
    outs = pl.pallas_call(
        write_out,
        out_shape=out_shape,
        in_specs=[hbm] * 7,
        out_specs=[hbm] * 7,
        scratch_shapes=[pltpu.VMEM(out.shape, out.dtype) for out in out_shape]
        + [dma((7,)), dma((7,))],
        compiler_params=pltpu.CompilerParams(vmem_limit_bytes=vmem_limit),
        name="write_results",
    )(*outs)
    return (outs[0].reshape(node_feat.shape), *outs[1:])


def solution(mesh):
    in_specs = (
        P("dom", "sub", None),
        P(("dom", "sub"), None),
        P(("dom", "sub")),
        P(("dom", "sub")),
        P(("dom", "sub")),
        P("dom", None),
        P("dom", None),
        P("dom", None),
        P("dom", None),
        P(None, "dom"),
        P("dom", "sub", None),
        P(("dom", "sub"), None),
    )
    out_specs = (
        P("dom", "sub", None),
        P(("dom", "sub"), None),
        P("dom", None),
        P("dom", None),
        P("dom", None),
        P("dom", None),
        P(None, "dom"),
    )
    return jax.shard_map(shards, mesh=mesh, in_specs=in_specs, out_specs=out_specs, check_vma=False)
```

```python
import functools

import jax
import jax.numpy as jnp
from jax import lax
from jax.experimental import pallas as pl
from jax.experimental.pallas import tpu as pltpu
from jax.sharding import PartitionSpec as P

MESH = pl.DeviceIdType.MESH
BF = jnp.bfloat16
F32 = jnp.float32
LANES = 128


def ceil_to(value, step):
    return -(-value // step) * step


def mm(a, b):
    return jnp.dot(a, b, preferred_element_type=F32)


def mm_nt(a, b):
    return lax.dot_general(a, b, (((1,), (1,)), ((), ())), preferred_element_type=F32)


def mm_tn(a, b):
    return lax.dot_general(a, b, (((0,), (0,)), ((), ())), preferred_element_type=F32)


def iota(shape, dim):
    return lax.broadcasted_iota(jnp.int32, shape, dim)


def one_hot(mask):
    return jnp.where(mask, 1.0, 0.0).astype(BF)


def layer_norm(raw_out):
    average = jnp.mean(raw_out, axis=-1, keepdims=True)
    centered = raw_out - average
    inv_std = lax.rsqrt(jnp.mean(centered * centered, axis=-1, keepdims=True) + 1e-05)
    return centered * inv_std, inv_std


def norm_back(upstream, normed, inv_std):
    return (
        upstream
        - jnp.mean(upstream, axis=-1, keepdims=True)
        - normed * jnp.mean(upstream * normed, axis=-1, keepdims=True)
    ) * inv_std


def each_chunk(total, step, body, init=0):
    carry = init
    for at in range(0, total, step):
        carry = body(slice(at, at + step), at, carry)
    return carry


class Plan:
    def __init__(self, n_dom, n_sub, side, edges, latent, rows):
        self.n_dom, self.n_sub = n_dom, n_sub
        self.side, self.edges, self.latent = side, edges, latent
        self.nodes = side * side
        self.own = ceil_to(self.nodes, LANES)
        self.strip = ceil_to(side, 16)
        self.halo = ceil_to(4 * self.strip, LANES)
        self.rows = rows
        at = 0
        self.off = {}
        for name in ("node_in", "node_out", "edge_in", "edge_out", "gains"):
            self.off[name] = at
            at += 16 if name == "gains" else ceil_to(rows[name], 16)
        self.shard = at
        self.node_part = self.off["edge_in"]
        self.piece = ceil_to(-(-at // n_sub), 16)
        self.total = self.piece * n_sub


def kernel(
    plan,
    node_hbm,
    feat_hbm,
    dst_hbm,
    dir_hbm,
    count_ref,
    wei_hbm,
    weo_hbm,
    wni_hbm,
    wno_hbm,
    gains_hbm,
    ncot_hbm,
    ecot_hbm,
    node_out_hbm,
    edge_out_hbm,
    gei_out_hbm,
    geo_out_hbm,
    gni_out_hbm,
    gno_out_hbm,
    gain_out_hbm,
    node_out,
    edge_out,
    gei_out,
    geo_out,
    gni_out,
    gno_out,
    gain_out,
    out_sem,
    node_ref,
    feat_ref,
    dst_ref,
    dir_ref,
    wei_ref,
    weo_ref,
    wni_ref,
    wno_ref,
    gains_ref,
    ncot_ref,
    ecot_ref,
    in_sem,
    wbuf,
    table,
    strips,
    gstrips,
    ghalo,
    s_dst,
    s_src,
    t_dst,
    t_src,
    x_e,
    hid_e,
    normed_e,
    inv_e,
    gpre_e,
    graw_e,
    msg,
    agg,
    x_n,
    hid_n,
    graw_n,
    gpre_n,
    node_acc,
    g1,
    r1,
    p2,
    r2,
    fin,
    w_send,
    w_recv,
    v_send,
    v_recv,
    h_send,
    h_recv,
    b_send,
    b_recv,
    n_send,
    n_recv,
    e_send,
    e_recv,
    q_send,
    q_recv,
    f_send,
    f_recv,
):
    n_dom, n_sub, side, edges = plan.n_dom, plan.n_sub, plan.side, plan.edges
    nodes, n_own, strip, lat = plan.nodes, plan.own, plan.strip, plan.latent
    n_halo, off, rows = plan.halo, plan.off, plan.rows
    d = lax.axis_index("dom")
    s = lax.axis_index("sub")

    pairs = (
        (wei_hbm, wei_ref),
        (weo_hbm, weo_ref),
        (wni_hbm, wni_ref),
        (wno_hbm, wno_ref),
        (gains_hbm, gains_ref),
        (node_hbm, node_ref),
        (dst_hbm, dst_ref),
        (dir_hbm, dir_ref),
        (feat_hbm, feat_ref),
        (ncot_hbm, ncot_ref),
        (ecot_hbm, ecot_ref),
    )
    loads = [
        pltpu.make_async_copy(hbm, ref, in_sem.at[i]) for i, (hbm, ref) in enumerate(pairs)
    ]
    for load in loads:
        load.start()
    pairs = (
        (node_out, node_out_hbm),
        (edge_out, edge_out_hbm),
        (gei_out, gei_out_hbm),
        (geo_out, geo_out_hbm),
        (gni_out, gni_out_hbm),
        (gno_out, gno_out_hbm),
        (gain_out, gain_out_hbm),
    )
    stores = [
        pltpu.make_async_copy(ref, hbm, out_sem.at[i]) for i, (ref, hbm) in enumerate(pairs)
    ]

    table[n_own:, :] = jnp.zeros((n_halo, lat), BF)
    ghalo[...] = jnp.zeros_like(ghalo)
    barrier = pltpu.get_barrier_semaphore()
    for k in range(1, n_dom):
        pl.semaphore_signal(
            barrier, inc=1, device_id={"dom": lax.rem(d + k, n_dom)}, device_id_type=MESH
        )
    for k in range(1, n_sub):
        pl.semaphore_signal(
            barrier, inc=1, device_id={"sub": lax.rem(s + k, n_sub)}, device_id_type=MESH
        )

    for load in loads[:5]:
        load.wait()
    shard_refs = {"edge_in": wei_ref, "edge_out": weo_ref, "node_in": wni_ref, "node_out": wno_ref}
    for name, ref in shard_refs.items():
        wbuf[d, off[name] : off[name] + rows[name], :] = ref[...]
    width = gains_ref.shape[1]
    gains32 = gains_ref[...].astype(F32)
    row16 = iota((16, width), 0)
    gains16 = jnp.where(
        row16 == 0, gains32[0:1, :], jnp.where(row16 == 1, gains32[1:2, :], 0.0)
    ).astype(BF)
    place = one_hot(iota((width, lat), 1) == iota((width, lat), 0) + d * width)
    wbuf[d, off["gains"] : off["gains"] + 16, :] = mm(gains16, place).astype(BF)

    loads[5].wait()
    table[0:nodes, :] = node_ref[...]
    table[nodes:n_own, :] = jnp.zeros((n_own - nodes, lat), BF)
    pos = iota((strip, n_own), 0)
    node_id = iota((strip, n_own), 1)
    inside = pos < side
    borders = (pos, (side - 1) * side + pos, pos * side, pos * side + side - 1)
    for b in range(4):
        select = one_hot((node_id == borders[b]) & inside)
        strips[b * strip : (b + 1) * strip, :] = mm(select, table[0:n_own, :]).astype(BF)

    pl.semaphore_wait(barrier, (n_dom - 1) + (n_sub - 1))

    def weight_copies(first, last, send, recv):
        copies = []
        for k in range(1, n_dom):
            copy = pltpu.make_async_remote_copy(
                src_ref=wbuf.at[d, pl.ds(first, last - first)],
                dst_ref=wbuf.at[d, pl.ds(first, last - first)],
                send_sem=send.at[k],
                recv_sem=recv.at[k],
                device_id={"dom": lax.rem(d + k, n_dom)},
                device_id_type=MESH,
            )
            copy.start()
            copies.append(copy)
        return copies

    w_copies = weight_copies(plan.node_part, plan.shard, w_send, w_recv)

    low_d, high_d = d > 0, d < n_dom - 1
    low_s, high_s = s > 0, s < n_sub - 1
    down_d, up_d = {"dom": jnp.maximum(d - 1, 0)}, {"dom": jnp.minimum(d + 1, n_dom - 1)}
    down_s, up_s = {"sub": jnp.maximum(s - 1, 0)}, {"sub": jnp.minimum(s + 1, n_sub - 1)}

    def strip_copies(source, target, first, send, recv, devices):
        return [
            pltpu.make_async_remote_copy(
                src_ref=source.at[pl.ds(b * strip, strip)],
                dst_ref=target.at[pl.ds(first + b * strip, strip)],
                send_sem=send.at[b],
                recv_sem=recv.at[b],
                device_id=devices[b],
                device_id_type=MESH,
            )
            for b in range(4)
        ]

    def when_all(conditions, actions):
        for condition, action in zip(conditions, actions):
            pl.when(condition)(action)

    h_copies = strip_copies(strips, table, n_own, h_send, h_recv, (down_d, up_d, down_s, up_s))
    h_to, h_from = (low_d, high_d, low_s, high_s), (high_d, low_d, high_s, low_s)
    when_all(h_to, [c.start for c in h_copies])
    v_copies = weight_copies(0, plan.node_part, v_send, v_recv)

    for load in loads[6:9]:
        load.wait()
    count = count_ref[0]
    step = max(n for n in (128, 256, 512) if edges % n == 0)

    def indices(cut_e, at, carry):
        line = slice(at // LANES, at // LANES + 1)
        dst = dst_ref[line, :]
        direction = dir_ref[line, :]
        row = jnp.floor((dst.astype(F32) + 0.5) * (1.0 / side)).astype(jnp.int32)
        col = dst - row * side
        src = jnp.where(
            direction == 0,
            jnp.where(row == side - 1, n_own + col, dst + side),
            jnp.where(
                direction == 1,
                jnp.where(row == 0, n_own + strip + col, dst - side),
                jnp.where(
                    direction == 2,
                    jnp.where(col == side - 1, n_own + 2 * strip + row, dst + 1),
                    jnp.where(col == 0, n_own + 3 * strip + row, dst - 1),
                ),
            ),
        )
        dst = jnp.where(iota((1, LANES), 1) + at < count, dst, -1)
        dst_cols = jnp.broadcast_to(dst, (LANES, LANES)).T
        src_cols = jnp.broadcast_to(src, (LANES, LANES)).T
        lane = iota((LANES, LANES), 1)
        for t in range((n_own + n_halo) // LANES):
            cut = slice(t * LANES, (t + 1) * LANES)
            s_src[cut_e, cut] = one_hot(src_cols == lane + t * LANES)
            if t < n_own // LANES:
                s_dst[cut_e, cut] = one_hot(dst_cols == lane + t * LANES)
        t_src[:, cut_e] = one_hot(iota((n_own + n_halo, LANES), 0) == src)
        t_dst[:, cut_e] = one_hot(iota((n_own, LANES), 0) == dst)
        return carry

    each_chunk(edges, LANES, indices)
    x_e[:, 0:lat] = feat_ref[...]

    def gather_dst(cut, at, carry):
        x_e[cut, 2 * lat :] = mm(s_dst[cut, :], table[0:n_own, :]).astype(BF)
        return carry

    each_chunk(edges, step, gather_dst)
    when_all(h_from, [c.wait_recv for c in h_copies])

    def gather_src(cut, at, carry):
        x_e[cut, lat : 2 * lat] = mm(s_src[cut, :], table[...]).astype(BF)
        return carry

    each_chunk(edges, step, gather_src)
    for copy in w_copies:
        copy.wait_recv()

    def whole(name):
        at, size = off[name], rows[name]
        if size % 16 == 0:
            return jnp.concatenate([wbuf[n, at : at + size, :] for n in range(n_dom)], axis=0)
        padded = ceil_to(size, 16)
        parts = [wbuf[n, at : at + padded, :].astype(F32)[0:size, :] for n in range(n_dom)]
        return jnp.concatenate(parts, axis=0).astype(BF)

    w1e, w2e = whole("edge_in"), whole("edge_out")
    gains = sum(wbuf[n, off["gains"] : off["gains"] + 16, :].astype(F32) for n in range(n_dom))
    gain_edge, gain_node = gains[0:1, :], gains[1:2, :]

    def edge_forward(cut, at, carry):
        hidden = jnp.maximum(mm(x_e[cut, :], w1e), 0.0).astype(BF)
        hid_e[cut, :] = hidden
        normed, inv_std = layer_norm(mm(hidden, w2e))
        normed_e[cut, :] = normed
        inv_e[cut, :] = inv_std
        message = normed * gain_edge
        high = message.astype(BF)
        msg[cut, 0:lat] = high
        msg[cut, lat:] = (message - high.astype(F32)).astype(BF)
        return carry

    each_chunk(edges, step, edge_forward)
    both = mm(t_dst[...], msg[...])
    agg[...] = (both[:, 0:lat] + both[:, lat:]).astype(BF)

    for load in loads[9:]:
        load.wait()
    scale = (n_dom * n_sub * nodes) ** -0.5
    for copy in v_copies:
        copy.wait_recv()
    w1n, w2n = whole("node_in"), whole("node_out")
    x_n[:, 0:lat] = table[0:n_own, :]
    x_n[:, lat:] = agg[...]

    def node_both(cut, at, gain_sum):
        inputs = x_n[cut, :]
        hidden = jnp.maximum(mm(inputs, w1n), 0.0).astype(BF)
        normed, inv_std = layer_norm(mm(hidden, w2n))
        upstream = ncot_ref[cut, :].astype(F32)
        graw = norm_back(upstream * gain_node, normed, inv_std).astype(BF)
        gpre = jnp.where(hidden > 0, mm_nt(graw, w2n), 0.0).astype(BF)
        hid_n[cut, :] = hidden
        graw_n[cut, :] = graw
        gpre_n[cut, :] = gpre
        grad_in = mm_nt(gpre, w1n)
        node_acc[cut, :] = upstream + grad_in[:, 0:lat]
        agg[cut, :] = grad_in[:, lat:].astype(BF)
        return gain_sum + jnp.sum(upstream * normed, axis=0, keepdims=True)

    node_step = max(n for n in range(16, 289, 16) if nodes % n == 0)
    node_gain = each_chunk(nodes, node_step, node_both, jnp.zeros((1, lat), F32))

    def pack(name, value):
        size = rows[name]
        for n in range(n_dom):
            g1[n, off[name] : off[name] + size, :] = (
                value[n * size : (n + 1) * size, :] * scale
            ).astype(BF)
            if size % 16:
                end = off[name] + ceil_to(size, 16)
                g1[n, off[name] + size : end, :] = jnp.zeros((end - off[name] - size, lat), BF)

    def dom_copies(first, last, send, recv):
        copies = []
        for k in range(1, n_dom):
            peer = lax.rem(d + k, n_dom)
            copy = pltpu.make_async_remote_copy(
                src_ref=g1.at[peer, pl.ds(first, last - first)],
                dst_ref=r1.at[k, pl.ds(first, last - first)],
                send_sem=send.at[k],
                recv_sem=recv.at[k],
                device_id={"dom": peer},
                device_id_type=MESH,
            )
            copy.start()
            copies.append(copy)
        return copies

    pack("node_in", mm_tn(gpre_n[...], x_n[0:nodes, :]).T)
    pack("node_out", mm_tn(hid_n[...], graw_n[...]))
    n_copies = dom_copies(0, plan.node_part, n_send, n_recv)

    def edge_backward(cut, at, gain_sum):
        cot = ecot_ref[cut, :].astype(F32)
        live = iota((step, lat), 0) + at < count
        upstream = jnp.where(live, cot, 0.0) + mm(s_dst[cut, :], agg[...])
        normed, inv_std = normed_e[cut, :], inv_e[cut, :]
        graw = norm_back(upstream * gain_edge, normed, inv_std).astype(BF)
        graw_e[cut, :] = graw
        gpre_e[cut, :] = jnp.where(hid_e[cut, :] > 0, mm_nt(graw, w2e), 0.0).astype(BF)
        return gain_sum + jnp.sum(upstream * normed, axis=0, keepdims=True)

    edge_gain = each_chunk(edges, step, edge_backward, jnp.zeros((1, lat), F32))

    pack("edge_in", mm_tn(gpre_e[...], x_e[...]).T)
    pack("edge_out", mm_tn(hid_e[...], graw_e[...]))
    row16 = iota((16, lat), 0)
    gains16 = jnp.where(row16 == 0, edge_gain, jnp.where(row16 == 1, node_gain, 0.0))
    for n in range(n_dom):
        g1[n, off["gains"] : off["gains"] + 16, :] = (gains16 * scale).astype(BF)
        if plan.total > plan.shard:
            g1[n, plan.shard :, :] = jnp.zeros((plan.total - plan.shard, lat), BF)
    e_copies = dom_copies(plan.node_part, plan.total, e_send, e_recv)

    w_src, w_dst = w1e[lat : 2 * lat, :], w1e[2 * lat :, :]
    back = mm(t_src[n_own:, :], gpre_e[...]).astype(BF)
    gstrips[...] = mm_nt(back, w_src).astype(BF)
    b_copies = strip_copies(gstrips, ghalo, 0, b_send, b_recv, (up_d, down_d, up_s, down_s))
    when_all(h_from, [c.start for c in b_copies])


    def edge_result(cut, at, carry):
        grad = mm_nt(gpre_e[cut, :], w1e[0:lat, :])
        edge_out[cut, :] = (ecot_ref[cut, :].astype(F32) + grad).astype(BF)
        return carry

    each_chunk(edges, step, edge_result)
    stores[1].start()

    for copy in n_copies + e_copies:
        copy.wait_recv()
    acc = g1[d].astype(F32)
    for k in range(1, n_dom):
        acc = acc + r1[k].astype(F32)
    p2[...] = acc.astype(BF).reshape(n_sub, plan.piece, lat)
    q_copies = []
    for k in range(1, n_sub):
        peer = lax.rem(s + k, n_sub)
        copy = pltpu.make_async_remote_copy(
            src_ref=p2.at[peer],
            dst_ref=r2.at[k],
            send_sem=q_send.at[k],
            recv_sem=q_recv.at[k],
            device_id={"sub": peer},
            device_id_type=MESH,
        )
        copy.start()
        q_copies.append(copy)

    at_src = mm(t_src[0:n_own, :], gpre_e[...]).astype(BF)
    at_dst = mm(t_dst[...], gpre_e[...]).astype(BF)
    spread = mm_nt(at_src, w_src) + mm_nt(at_dst, w_dst)

    for copy in q_copies:
        copy.wait_recv()
    acc = p2[s].astype(F32)
    for k in range(1, n_sub):
        acc = acc + r2[k].astype(F32)
    fin[s] = acc.astype(BF)
    f_copies = []
    for k in range(1, n_sub):
        copy = pltpu.make_async_remote_copy(
            src_ref=fin.at[s],
            dst_ref=fin.at[s],
            send_sem=f_send.at[k],
            recv_sem=f_recv.at[k],
            device_id={"sub": lax.rem(s + k, n_sub)},
            device_id_type=MESH,
        )
        copy.start()
        f_copies.append(copy)
    when_all(h_to, [c.wait_recv for c in b_copies])
    pos = iota((n_own, n_halo), 1)
    node_id = iota((n_own, n_halo), 0)
    picked = jnp.zeros((n_own, n_halo), jnp.bool_)
    for b in range(4):
        at = pos - b * strip
        border = (at, (side - 1) * side + at, at * side, at * side + side - 1)[b]
        picked = picked | ((at >= 0) & (at < side) & (node_id == border))
    spread = spread + mm(one_hot(picked), ghalo[...])
    node_out[...] = (node_acc[...] + spread[0:nodes, :]).astype(BF)
    stores[0].start()

    for copy in f_copies:
        copy.wait_recv()
    result = fin[...].reshape(plan.total, lat)
    for name, ref in (
        ("edge_in", gei_out),
        ("edge_out", geo_out),
        ("node_in", gni_out),
        ("node_out", gno_out),
    ):
        ref[...] = result[off[name] : off[name] + ceil_to(rows[name], 16), :].astype(F32)[
            0 : rows[name], :
        ]
    gain_out[...] = mm_nt(result[off["gains"] : off["gains"] + 16, :], place)[0:2, :]
    for store in stores[2:]:
        store.start()

    for copy in w_copies + v_copies + n_copies + e_copies + q_copies + f_copies:
        copy.wait_send()
    when_all(h_to, [c.wait_send for c in h_copies])
    when_all(h_from, [c.wait_send for c in b_copies])
    for store in stores:
        store.wait()


def write_out(*refs):
    sources, targets, stage, in_sem, out_sem = refs[:7], refs[7:14], refs[14:21], *refs[21:]
    reads = [pltpu.make_async_copy(sources[i], stage[i], in_sem.at[i]) for i in range(7)]
    writes = [pltpu.make_async_copy(stage[i], targets[i], out_sem.at[i]) for i in range(7)]
    for read in reads:
        read.start()
    for read, write in zip(reads, writes):
        read.wait()
        write.start()
    for write in writes:
        write.wait()


def shards(
    node_feat,
    edge_feat,
    edge_dst,
    edge_dir,
    edge_count,
    w_edge_in,
    w_edge_out,
    w_node_in,
    w_node_out,
    gains,
    node_cot,
    edge_cot,
):
    n_dom, n_sub = lax.axis_size("dom"), lax.axis_size("sub")
    side, _, lat = node_feat.shape
    edges = edge_feat.shape[0]
    rows = {
        "edge_in": w_edge_in.shape[0],
        "edge_out": w_edge_out.shape[0],
        "node_in": w_node_in.shape[0],
        "node_out": w_node_out.shape[0],
    }
    plan = Plan(n_dom, n_sub, side, edges, lat, rows)
    nodes, n_own, n_halo = plan.nodes, plan.own, plan.halo
    table = n_own + n_halo
    dma = pltpu.SemaphoreType.DMA
    hbm = pl.BlockSpec(memory_space=pltpu.HBM)
    vmem_limit = 64 * 1024 * 1024
    out_shape = [
        jax.ShapeDtypeStruct((nodes, lat), BF),
        jax.ShapeDtypeStruct((edges, lat), BF),
        jax.ShapeDtypeStruct(w_edge_in.shape, F32),
        jax.ShapeDtypeStruct(w_edge_out.shape, F32),
        jax.ShapeDtypeStruct(w_node_in.shape, F32),
        jax.ShapeDtypeStruct(w_node_out.shape, F32),
        jax.ShapeDtypeStruct(gains.shape, F32),
    ]
    outs = pl.pallas_call(
        functools.partial(kernel, plan),
        out_shape=out_shape,
        in_specs=[hbm] * 4 + [pl.BlockSpec(memory_space=pltpu.SMEM)] + [hbm] * 7,
        out_specs=[hbm] * 7,
        scratch_shapes=[pltpu.VMEM(out.shape, out.dtype) for out in out_shape]
        + [
            dma((7,)),
            pltpu.VMEM((nodes, lat), BF),
            pltpu.VMEM((edges, lat), BF),
            pltpu.VMEM((edges // LANES, LANES), jnp.int32),
            pltpu.VMEM((edges // LANES, LANES), jnp.int32),
            pltpu.VMEM(w_edge_in.shape, BF),
            pltpu.VMEM(w_edge_out.shape, BF),
            pltpu.VMEM(w_node_in.shape, BF),
            pltpu.VMEM(w_node_out.shape, BF),
            pltpu.VMEM(gains.shape, BF),
            pltpu.VMEM((nodes, lat), BF),
            pltpu.VMEM((edges, lat), BF),
            dma((11,)),
            pltpu.VMEM((n_dom, plan.shard, lat), BF),
            pltpu.VMEM((table, lat), BF),
            pltpu.VMEM((n_halo, lat), BF),
            pltpu.VMEM((n_halo, lat), BF),
            pltpu.VMEM((n_halo, lat), BF),
            pltpu.VMEM((edges, n_own), BF),
            pltpu.VMEM((edges, table), BF),
            pltpu.VMEM((n_own, edges), BF),
            pltpu.VMEM((table, edges), BF),
            pltpu.VMEM((edges, 3 * lat), BF),
            pltpu.VMEM((edges, lat), BF),
            pltpu.VMEM((edges, lat), F32),
            pltpu.VMEM((edges, 1), F32),
            pltpu.VMEM((edges, lat), BF),
            pltpu.VMEM((edges, lat), BF),
            pltpu.VMEM((edges, 2 * lat), BF),
            pltpu.VMEM((n_own, lat), BF),
            pltpu.VMEM((n_own, 2 * lat), BF),
            pltpu.VMEM((nodes, lat), BF),
            pltpu.VMEM((nodes, lat), BF),
            pltpu.VMEM((nodes, lat), BF),
            pltpu.VMEM((nodes, lat), F32),
            pltpu.VMEM((n_dom, plan.total, lat), BF),
            pltpu.VMEM((n_dom, plan.total, lat), BF),
            pltpu.VMEM((n_sub, plan.piece, lat), BF),
            pltpu.VMEM((n_sub, plan.piece, lat), BF),
            pltpu.VMEM((n_sub, plan.piece, lat), BF),
            dma((n_dom,)),
            dma((n_dom,)),
            dma((n_dom,)),
            dma((n_dom,)),
            dma((4,)),
            dma((4,)),
            dma((4,)),
            dma((4,)),
            dma((n_dom,)),
            dma((n_dom,)),
            dma((n_dom,)),
            dma((n_dom,)),
            dma((n_sub,)),
            dma((n_sub,)),
            dma((n_sub,)),
            dma((n_sub,)),
        ],
        compiler_params=pltpu.CompilerParams(
            collective_id=0, has_side_effects=True, vmem_limit_bytes=vmem_limit
        ),
        name="graph_layer_backward",
    )(
        node_feat.reshape(nodes, lat),
        edge_feat,
        edge_dst.reshape(edges // LANES, LANES),
        edge_dir.reshape(edges // LANES, LANES),
        edge_count,
        w_edge_in,
        w_edge_out,
        w_node_in,
        w_node_out,
        gains,
        node_cot.reshape(nodes, lat),
        edge_cot,
    )
    outs = pl.pallas_call(
        write_out,
        out_shape=out_shape,
        in_specs=[hbm] * 7,
        out_specs=[hbm] * 7,
        scratch_shapes=[pltpu.VMEM(out.shape, out.dtype) for out in out_shape]
        + [dma((7,)), dma((7,))],
        compiler_params=pltpu.CompilerParams(vmem_limit_bytes=vmem_limit),
        name="write_results",
    )(*outs)
    return (outs[0].reshape(node_feat.shape), *outs[1:])


def solution(mesh):
    in_specs = (
        P("dom", "sub", None),
        P(("dom", "sub"), None),
        P(("dom", "sub")),
        P(("dom", "sub")),
        P(("dom", "sub")),
        P("dom", None),
        P("dom", None),
        P("dom", None),
        P("dom", None),
        P(None, "dom"),
        P("dom", "sub", None),
        P(("dom", "sub"), None),
    )
    out_specs = (
        P("dom", "sub", None),
        P(("dom", "sub"), None),
        P("dom", None),
        P("dom", None),
        P("dom", None),
        P("dom", None),
        P(None, "dom"),
    )
    return jax.shard_map(shards, mesh=mesh, in_specs=in_specs, out_specs=out_specs, check_vma=False)
```

```python
import functools

import jax
import jax.numpy as jnp
from jax import lax
from jax.experimental import pallas as pl
from jax.experimental.pallas import tpu as pltpu
from jax.sharding import PartitionSpec as P

MESH = pl.DeviceIdType.MESH
BF = jnp.bfloat16
F32 = jnp.float32
LANES = 128


def ceil_to(value, step):
    return -(-value // step) * step


def mm(a, b):
    return jnp.dot(a, b, preferred_element_type=F32)


def mm_nt(a, b):
    return lax.dot_general(a, b, (((1,), (1,)), ((), ())), preferred_element_type=F32)


def mm_tn(a, b):
    return lax.dot_general(a, b, (((0,), (0,)), ((), ())), preferred_element_type=F32)


def iota(shape, dim):
    return lax.broadcasted_iota(jnp.int32, shape, dim)


def one_hot(mask):
    return jnp.where(mask, 1.0, 0.0).astype(BF)


def layer_norm(raw_out):
    average = jnp.mean(raw_out, axis=-1, keepdims=True)
    centered = raw_out - average
    inv_std = lax.rsqrt(jnp.mean(centered * centered, axis=-1, keepdims=True) + 1e-05)
    return centered * inv_std, inv_std


def norm_back(upstream, normed, inv_std):
    return (
        upstream
        - jnp.mean(upstream, axis=-1, keepdims=True)
        - normed * jnp.mean(upstream * normed, axis=-1, keepdims=True)
    ) * inv_std


def each_chunk(total, step, body, init=0):
    carry = init
    for at in range(0, total, step):
        carry = body(slice(at, at + step), at, carry)
    return carry


class Plan:
    def __init__(self, n_dom, n_sub, side, edges, latent, rows):
        self.n_dom, self.n_sub = n_dom, n_sub
        self.side, self.edges, self.latent = side, edges, latent
        self.nodes = side * side
        self.own = ceil_to(self.nodes, LANES)
        self.strip = ceil_to(side, 16)
        self.halo = ceil_to(4 * self.strip, LANES)
        self.rows = rows
        at = 0
        self.off = {}
        for name in ("node_in", "node_out", "edge_in", "edge_out", "gains"):
            self.off[name] = at
            at += 16 if name == "gains" else ceil_to(rows[name], 16)
        self.shard = at
        self.node_part = self.off["edge_in"]
        self.piece = ceil_to(-(-at // n_sub), 16)
        self.total = self.piece * n_sub


def kernel(
    plan,
    node_hbm,
    feat_hbm,
    dst_hbm,
    dir_hbm,
    count_ref,
    wei_hbm,
    weo_hbm,
    wni_hbm,
    wno_hbm,
    gains_hbm,
    ncot_hbm,
    ecot_hbm,
    node_out_hbm,
    edge_out_hbm,
    gei_out_hbm,
    geo_out_hbm,
    gni_out_hbm,
    gno_out_hbm,
    gain_out_hbm,
    node_out,
    edge_out,
    gei_out,
    geo_out,
    gni_out,
    gno_out,
    gain_out,
    out_sem,
    node_ref,
    feat_ref,
    dst_ref,
    dir_ref,
    wei_ref,
    weo_ref,
    wni_ref,
    wno_ref,
    gains_ref,
    ncot_ref,
    ecot_ref,
    in_sem,
    wbuf,
    table,
    strips,
    gstrips,
    ghalo,
    s_dst,
    s_src,
    t_dst,
    t_src,
    x_e,
    hid_e,
    normed_e,
    inv_e,
    gpre_e,
    graw_e,
    msg,
    agg,
    x_n,
    hid_n,
    graw_n,
    gpre_n,
    node_acc,
    g1,
    r1,
    p2,
    r2,
    fin,
    w_send,
    w_recv,
    v_send,
    v_recv,
    h_send,
    h_recv,
    b_send,
    b_recv,
    n_send,
    n_recv,
    e_send,
    e_recv,
    q_send,
    q_recv,
    f_send,
    f_recv,
):
    n_dom, n_sub, side, edges = plan.n_dom, plan.n_sub, plan.side, plan.edges
    nodes, n_own, strip, lat = plan.nodes, plan.own, plan.strip, plan.latent
    n_halo, off, rows = plan.halo, plan.off, plan.rows
    d = lax.axis_index("dom")
    s = lax.axis_index("sub")

    pairs = (
        (wei_hbm, wei_ref),
        (weo_hbm, weo_ref),
        (wni_hbm, wni_ref),
        (wno_hbm, wno_ref),
        (gains_hbm, gains_ref),
        (node_hbm, node_ref),
        (dst_hbm, dst_ref),
        (dir_hbm, dir_ref),
        (feat_hbm, feat_ref),
        (ncot_hbm, ncot_ref),
        (ecot_hbm, ecot_ref),
    )
    loads = [
        pltpu.make_async_copy(hbm, ref, in_sem.at[i]) for i, (hbm, ref) in enumerate(pairs)
    ]
    for load in loads:
        load.start()
    pairs = (
        (node_out, node_out_hbm),
        (edge_out, edge_out_hbm),
        (gei_out, gei_out_hbm),
        (geo_out, geo_out_hbm),
        (gni_out, gni_out_hbm),
        (gno_out, gno_out_hbm),
        (gain_out, gain_out_hbm),
    )
    stores = [
        pltpu.make_async_copy(ref, hbm, out_sem.at[i]) for i, (ref, hbm) in enumerate(pairs)
    ]

    table[n_own:, :] = jnp.zeros((n_halo, lat), BF)
    ghalo[...] = jnp.zeros_like(ghalo)
    barrier = pltpu.get_barrier_semaphore()
    for k in range(1, n_dom):
        pl.semaphore_signal(
            barrier, inc=1, device_id={"dom": lax.rem(d + k, n_dom)}, device_id_type=MESH
        )
    for k in range(1, n_sub):
        pl.semaphore_signal(
            barrier, inc=1, device_id={"sub": lax.rem(s + k, n_sub)}, device_id_type=MESH
        )

    for load in loads[:5]:
        load.wait()
    shard_refs = {"edge_in": wei_ref, "edge_out": weo_ref, "node_in": wni_ref, "node_out": wno_ref}
    for name, ref in shard_refs.items():
        wbuf[d, off[name] : off[name] + rows[name], :] = ref[...]
    width = gains_ref.shape[1]
    gains32 = gains_ref[...].astype(F32)
    row16 = iota((16, width), 0)
    gains16 = jnp.where(
        row16 == 0, gains32[0:1, :], jnp.where(row16 == 1, gains32[1:2, :], 0.0)
    ).astype(BF)
    place = one_hot(iota((width, lat), 1) == iota((width, lat), 0) + d * width)
    wbuf[d, off["gains"] : off["gains"] + 16, :] = mm(gains16, place).astype(BF)

    loads[5].wait()
    table[0:nodes, :] = node_ref[...]
    table[nodes:n_own, :] = jnp.zeros((n_own - nodes, lat), BF)
    pos = iota((strip, n_own), 0)
    node_id = iota((strip, n_own), 1)
    inside = pos < side
    borders = (pos, (side - 1) * side + pos, pos * side, pos * side + side - 1)
    for b in range(4):
        select = one_hot((node_id == borders[b]) & inside)
        strips[b * strip : (b + 1) * strip, :] = mm(select, table[0:n_own, :]).astype(BF)

    pl.semaphore_wait(barrier, (n_dom - 1) + (n_sub - 1))

    def weight_copies(first, last, send, recv):
        copies = []
        for k in range(1, n_dom):
            copy = pltpu.make_async_remote_copy(
                src_ref=wbuf.at[d, pl.ds(first, last - first)],
                dst_ref=wbuf.at[d, pl.ds(first, last - first)],
                send_sem=send.at[k],
                recv_sem=recv.at[k],
                device_id={"dom": lax.rem(d + k, n_dom)},
                device_id_type=MESH,
            )
            copy.start()
            copies.append(copy)
        return copies

    w_copies = weight_copies(plan.node_part, plan.shard, w_send, w_recv)

    low_d, high_d = d > 0, d < n_dom - 1
    low_s, high_s = s > 0, s < n_sub - 1
    down_d, up_d = {"dom": jnp.maximum(d - 1, 0)}, {"dom": jnp.minimum(d + 1, n_dom - 1)}
    down_s, up_s = {"sub": jnp.maximum(s - 1, 0)}, {"sub": jnp.minimum(s + 1, n_sub - 1)}

    def strip_copies(source, target, first, send, recv, devices):
        return [
            pltpu.make_async_remote_copy(
                src_ref=source.at[pl.ds(b * strip, strip)],
                dst_ref=target.at[pl.ds(first + b * strip, strip)],
                send_sem=send.at[b],
                recv_sem=recv.at[b],
                device_id=devices[b],
                device_id_type=MESH,
            )
            for b in range(4)
        ]

    def when_all(conditions, actions):
        for condition, action in zip(conditions, actions):
            pl.when(condition)(action)

    h_copies = strip_copies(strips, table, n_own, h_send, h_recv, (down_d, up_d, down_s, up_s))
    h_to, h_from = (low_d, high_d, low_s, high_s), (high_d, low_d, high_s, low_s)
    when_all(h_to, [c.start for c in h_copies])
    v_copies = weight_copies(0, plan.node_part, v_send, v_recv)

    for load in loads[6:9]:
        load.wait()
    count = count_ref[0]
    step = max(n for n in (128, 256, 512, 1024) if edges % n == 0)

    def indices(cut_e, at, carry):
        line = slice(at // LANES, at // LANES + 1)
        dst = dst_ref[line, :]
        direction = dir_ref[line, :]
        row = jnp.floor((dst.astype(F32) + 0.5) * (1.0 / side)).astype(jnp.int32)
        col = dst - row * side
        src = jnp.where(
            direction == 0,
            jnp.where(row == side - 1, n_own + col, dst + side),
            jnp.where(
                direction == 1,
                jnp.where(row == 0, n_own + strip + col, dst - side),
                jnp.where(
                    direction == 2,
                    jnp.where(col == side - 1, n_own + 2 * strip + row, dst + 1),
                    jnp.where(col == 0, n_own + 3 * strip + row, dst - 1),
                ),
            ),
        )
        dst = jnp.where(iota((1, LANES), 1) + at < count, dst, -1)
        dst_cols = jnp.broadcast_to(dst, (LANES, LANES)).T
        src_cols = jnp.broadcast_to(src, (LANES, LANES)).T
        lane = iota((LANES, LANES), 1)
        for t in range((n_own + n_halo) // LANES):
            cut = slice(t * LANES, (t + 1) * LANES)
            s_src[cut_e, cut] = one_hot(src_cols == lane + t * LANES)
            if t < n_own // LANES:
                s_dst[cut_e, cut] = one_hot(dst_cols == lane + t * LANES)
        t_src[:, cut_e] = one_hot(iota((n_own + n_halo, LANES), 0) == src)
        t_dst[:, cut_e] = one_hot(iota((n_own, LANES), 0) == dst)
        return carry

    each_chunk(edges, LANES, indices)
    x_e[:, 0:lat] = feat_ref[...]

    def gather_dst(cut, at, carry):
        x_e[cut, 2 * lat :] = mm(s_dst[cut, :], table[0:n_own, :]).astype(BF)
        return carry

    each_chunk(edges, step, gather_dst)
    when_all(h_from, [c.wait_recv for c in h_copies])

    def gather_src(cut, at, carry):
        x_e[cut, lat : 2 * lat] = mm(s_src[cut, :], table[...]).astype(BF)
        return carry

    each_chunk(edges, step, gather_src)
    for copy in w_copies:
        copy.wait_recv()

    def whole(name):
        at, size = off[name], rows[name]
        if size % 16 == 0:
            return jnp.concatenate([wbuf[n, at : at + size, :] for n in range(n_dom)], axis=0)
        padded = ceil_to(size, 16)
        parts = [wbuf[n, at : at + padded, :].astype(F32)[0:size, :] for n in range(n_dom)]
        return jnp.concatenate(parts, axis=0).astype(BF)

    w1e, w2e = whole("edge_in"), whole("edge_out")
    gains = sum(wbuf[n, off["gains"] : off["gains"] + 16, :].astype(F32) for n in range(n_dom))
    gain_edge, gain_node = gains[0:1, :], gains[1:2, :]

    def edge_forward(cut, at, carry):
        hidden = jnp.maximum(mm(x_e[cut, :], w1e), 0.0).astype(BF)
        hid_e[cut, :] = hidden
        normed, inv_std = layer_norm(mm(hidden, w2e))
        normed_e[cut, :] = normed
        inv_e[cut, :] = inv_std
        message = normed * gain_edge
        high = message.astype(BF)
        msg[cut, 0:lat] = high
        msg[cut, lat:] = (message - high.astype(F32)).astype(BF)
        return carry

    each_chunk(edges, step, edge_forward)
    both = mm(t_dst[...], msg[...])
    agg[...] = (both[:, 0:lat] + both[:, lat:]).astype(BF)

    for load in loads[9:]:
        load.wait()
    scale = (n_dom * n_sub * nodes) ** -0.5
    for copy in v_copies:
        copy.wait_recv()
    w1n, w2n = whole("node_in"), whole("node_out")
    x_n[:, 0:lat] = table[0:n_own, :]
    x_n[:, lat:] = agg[...]

    def node_both(cut, at, gain_sum):
        inputs = x_n[cut, :]
        hidden = jnp.maximum(mm(inputs, w1n), 0.0).astype(BF)
        normed, inv_std = layer_norm(mm(hidden, w2n))
        upstream = ncot_ref[cut, :].astype(F32)
        graw = norm_back(upstream * gain_node, normed, inv_std).astype(BF)
        gpre = jnp.where(hidden > 0, mm_nt(graw, w2n), 0.0).astype(BF)
        hid_n[cut, :] = hidden
        graw_n[cut, :] = graw
        gpre_n[cut, :] = gpre
        grad_in = mm_nt(gpre, w1n)
        node_acc[cut, :] = upstream + grad_in[:, 0:lat]
        agg[cut, :] = grad_in[:, lat:].astype(BF)
        return gain_sum + jnp.sum(upstream * normed, axis=0, keepdims=True)

    node_step = max(n for n in range(16, 577, 16) if nodes % n == 0)
    node_gain = each_chunk(nodes, node_step, node_both, jnp.zeros((1, lat), F32))

    def pack(name, value):
        size = rows[name]
        for n in range(n_dom):
            g1[n, off[name] : off[name] + size, :] = (
                value[n * size : (n + 1) * size, :] * scale
            ).astype(BF)
            if size % 16:
                end = off[name] + ceil_to(size, 16)
                g1[n, off[name] + size : end, :] = jnp.zeros((end - off[name] - size, lat), BF)

    def dom_copies(first, last, send, recv):
        copies = []
        for k in range(1, n_dom):
            peer = lax.rem(d + k, n_dom)
            copy = pltpu.make_async_remote_copy(
                src_ref=g1.at[peer, pl.ds(first, last - first)],
                dst_ref=r1.at[k, pl.ds(first, last - first)],
                send_sem=send.at[k],
                recv_sem=recv.at[k],
                device_id={"dom": peer},
                device_id_type=MESH,
            )
            copy.start()
            copies.append(copy)
        return copies

    pack("node_in", mm_tn(gpre_n[...], x_n[0:nodes, :]).T)
    pack("node_out", mm_tn(hid_n[...], graw_n[...]))
    n_copies = dom_copies(0, plan.node_part, n_send, n_recv)

    def edge_backward(cut, at, gain_sum):
        cot = ecot_ref[cut, :].astype(F32)
        live = iota((step, lat), 0) + at < count
        upstream = jnp.where(live, cot, 0.0) + mm(s_dst[cut, :], agg[...])
        normed, inv_std = normed_e[cut, :], inv_e[cut, :]
        graw = norm_back(upstream * gain_edge, normed, inv_std).astype(BF)
        graw_e[cut, :] = graw
        gpre_e[cut, :] = jnp.where(hid_e[cut, :] > 0, mm_nt(graw, w2e), 0.0).astype(BF)
        return gain_sum + jnp.sum(upstream * normed, axis=0, keepdims=True)

    edge_gain = each_chunk(edges, step, edge_backward, jnp.zeros((1, lat), F32))

    pack("edge_in", mm_tn(gpre_e[...], x_e[...]).T)
    pack("edge_out", mm_tn(hid_e[...], graw_e[...]))
    row16 = iota((16, lat), 0)
    gains16 = jnp.where(row16 == 0, edge_gain, jnp.where(row16 == 1, node_gain, 0.0))
    for n in range(n_dom):
        g1[n, off["gains"] : off["gains"] + 16, :] = (gains16 * scale).astype(BF)
        if plan.total > plan.shard:
            g1[n, plan.shard :, :] = jnp.zeros((plan.total - plan.shard, lat), BF)
    e_copies = dom_copies(plan.node_part, plan.total, e_send, e_recv)

    w_src, w_dst = w1e[lat : 2 * lat, :], w1e[2 * lat :, :]
    back = mm(t_src[n_own:, :], gpre_e[...]).astype(BF)
    gstrips[...] = mm_nt(back, w_src).astype(BF)
    b_copies = strip_copies(gstrips, ghalo, 0, b_send, b_recv, (up_d, down_d, up_s, down_s))
    when_all(h_from, [c.start for c in b_copies])


    def edge_result(cut, at, carry):
        grad = mm_nt(gpre_e[cut, :], w1e[0:lat, :])
        edge_out[cut, :] = (ecot_ref[cut, :].astype(F32) + grad).astype(BF)
        return carry

    each_chunk(edges, step, edge_result)
    stores[1].start()

    for copy in n_copies + e_copies:
        copy.wait_recv()
    acc = g1[d].astype(F32)
    for k in range(1, n_dom):
        acc = acc + r1[k].astype(F32)
    p2[...] = acc.astype(BF).reshape(n_sub, plan.piece, lat)
    q_copies = []
    for k in range(1, n_sub):
        peer = lax.rem(s + k, n_sub)
        copy = pltpu.make_async_remote_copy(
            src_ref=p2.at[peer],
            dst_ref=r2.at[k],
            send_sem=q_send.at[k],
            recv_sem=q_recv.at[k],
            device_id={"sub": peer},
            device_id_type=MESH,
        )
        copy.start()
        q_copies.append(copy)

    at_src = mm(t_src[0:n_own, :], gpre_e[...]).astype(BF)
    at_dst = mm(t_dst[...], gpre_e[...]).astype(BF)
    spread = mm_nt(at_src, w_src) + mm_nt(at_dst, w_dst)

    for copy in q_copies:
        copy.wait_recv()
    acc = p2[s].astype(F32)
    for k in range(1, n_sub):
        acc = acc + r2[k].astype(F32)
    fin[s] = acc.astype(BF)
    f_copies = []
    for k in range(1, n_sub):
        copy = pltpu.make_async_remote_copy(
            src_ref=fin.at[s],
            dst_ref=fin.at[s],
            send_sem=f_send.at[k],
            recv_sem=f_recv.at[k],
            device_id={"sub": lax.rem(s + k, n_sub)},
            device_id_type=MESH,
        )
        copy.start()
        f_copies.append(copy)
    when_all(h_to, [c.wait_recv for c in b_copies])
    pos = iota((n_own, n_halo), 1)
    node_id = iota((n_own, n_halo), 0)
    picked = jnp.zeros((n_own, n_halo), jnp.bool_)
    for b in range(4):
        at = pos - b * strip
        border = (at, (side - 1) * side + at, at * side, at * side + side - 1)[b]
        picked = picked | ((at >= 0) & (at < side) & (node_id == border))
    spread = spread + mm(one_hot(picked), ghalo[...])
    node_out[...] = (node_acc[...] + spread[0:nodes, :]).astype(BF)
    stores[0].start()

    for copy in f_copies:
        copy.wait_recv()
    result = fin[...].reshape(plan.total, lat)
    for name, ref in (
        ("edge_in", gei_out),
        ("edge_out", geo_out),
        ("node_in", gni_out),
        ("node_out", gno_out),
    ):
        ref[...] = result[off[name] : off[name] + ceil_to(rows[name], 16), :].astype(F32)[
            0 : rows[name], :
        ]
    gain_out[...] = mm_nt(result[off["gains"] : off["gains"] + 16, :], place)[0:2, :]
    for store in stores[2:]:
        store.start()

    for copy in w_copies + v_copies + n_copies + e_copies + q_copies + f_copies:
        copy.wait_send()
    when_all(h_to, [c.wait_send for c in h_copies])
    when_all(h_from, [c.wait_send for c in b_copies])
    for store in stores:
        store.wait()


def write_out(*refs):
    sources, targets, stage, in_sem, out_sem = refs[:7], refs[7:14], refs[14:21], *refs[21:]
    reads = [pltpu.make_async_copy(sources[i], stage[i], in_sem.at[i]) for i in range(7)]
    writes = [pltpu.make_async_copy(stage[i], targets[i], out_sem.at[i]) for i in range(7)]
    for read in reads:
        read.start()
    for read, write in zip(reads, writes):
        read.wait()
        write.start()
    for write in writes:
        write.wait()


def shards(
    node_feat,
    edge_feat,
    edge_dst,
    edge_dir,
    edge_count,
    w_edge_in,
    w_edge_out,
    w_node_in,
    w_node_out,
    gains,
    node_cot,
    edge_cot,
):
    n_dom, n_sub = lax.axis_size("dom"), lax.axis_size("sub")
    side, _, lat = node_feat.shape
    edges = edge_feat.shape[0]
    rows = {
        "edge_in": w_edge_in.shape[0],
        "edge_out": w_edge_out.shape[0],
        "node_in": w_node_in.shape[0],
        "node_out": w_node_out.shape[0],
    }
    plan = Plan(n_dom, n_sub, side, edges, lat, rows)
    nodes, n_own, n_halo = plan.nodes, plan.own, plan.halo
    table = n_own + n_halo
    dma = pltpu.SemaphoreType.DMA
    hbm = pl.BlockSpec(memory_space=pltpu.HBM)
    vmem_limit = 64 * 1024 * 1024
    out_shape = [
        jax.ShapeDtypeStruct((nodes, lat), BF),
        jax.ShapeDtypeStruct((edges, lat), BF),
        jax.ShapeDtypeStruct(w_edge_in.shape, F32),
        jax.ShapeDtypeStruct(w_edge_out.shape, F32),
        jax.ShapeDtypeStruct(w_node_in.shape, F32),
        jax.ShapeDtypeStruct(w_node_out.shape, F32),
        jax.ShapeDtypeStruct(gains.shape, F32),
    ]
    outs = pl.pallas_call(
        functools.partial(kernel, plan),
        out_shape=out_shape,
        in_specs=[hbm] * 4 + [pl.BlockSpec(memory_space=pltpu.SMEM)] + [hbm] * 7,
        out_specs=[hbm] * 7,
        scratch_shapes=[pltpu.VMEM(out.shape, out.dtype) for out in out_shape]
        + [
            dma((7,)),
            pltpu.VMEM((nodes, lat), BF),
            pltpu.VMEM((edges, lat), BF),
            pltpu.VMEM((edges // LANES, LANES), jnp.int32),
            pltpu.VMEM((edges // LANES, LANES), jnp.int32),
            pltpu.VMEM(w_edge_in.shape, BF),
            pltpu.VMEM(w_edge_out.shape, BF),
            pltpu.VMEM(w_node_in.shape, BF),
            pltpu.VMEM(w_node_out.shape, BF),
            pltpu.VMEM(gains.shape, BF),
            pltpu.VMEM((nodes, lat), BF),
            pltpu.VMEM((edges, lat), BF),
            dma((11,)),
            pltpu.VMEM((n_dom, plan.shard, lat), BF),
            pltpu.VMEM((table, lat), BF),
            pltpu.VMEM((n_halo, lat), BF),
            pltpu.VMEM((n_halo, lat), BF),
            pltpu.VMEM((n_halo, lat), BF),
            pltpu.VMEM((edges, n_own), BF),
            pltpu.VMEM((edges, table), BF),
            pltpu.VMEM((n_own, edges), BF),
            pltpu.VMEM((table, edges), BF),
            pltpu.VMEM((edges, 3 * lat), BF),
            pltpu.VMEM((edges, lat), BF),
            pltpu.VMEM((edges, lat), F32),
            pltpu.VMEM((edges, 1), F32),
            pltpu.VMEM((edges, lat), BF),
            pltpu.VMEM((edges, lat), BF),
            pltpu.VMEM((edges, 2 * lat), BF),
            pltpu.VMEM((n_own, lat), BF),
            pltpu.VMEM((n_own, 2 * lat), BF),
            pltpu.VMEM((nodes, lat), BF),
            pltpu.VMEM((nodes, lat), BF),
            pltpu.VMEM((nodes, lat), BF),
            pltpu.VMEM((nodes, lat), F32),
            pltpu.VMEM((n_dom, plan.total, lat), BF),
            pltpu.VMEM((n_dom, plan.total, lat), BF),
            pltpu.VMEM((n_sub, plan.piece, lat), BF),
            pltpu.VMEM((n_sub, plan.piece, lat), BF),
            pltpu.VMEM((n_sub, plan.piece, lat), BF),
            dma((n_dom,)),
            dma((n_dom,)),
            dma((n_dom,)),
            dma((n_dom,)),
            dma((4,)),
            dma((4,)),
            dma((4,)),
            dma((4,)),
            dma((n_dom,)),
            dma((n_dom,)),
            dma((n_dom,)),
            dma((n_dom,)),
            dma((n_sub,)),
            dma((n_sub,)),
            dma((n_sub,)),
            dma((n_sub,)),
        ],
        compiler_params=pltpu.CompilerParams(
            collective_id=0, has_side_effects=True, vmem_limit_bytes=vmem_limit
        ),
        name="graph_layer_backward",
    )(
        node_feat.reshape(nodes, lat),
        edge_feat,
        edge_dst.reshape(edges // LANES, LANES),
        edge_dir.reshape(edges // LANES, LANES),
        edge_count,
        w_edge_in,
        w_edge_out,
        w_node_in,
        w_node_out,
        gains,
        node_cot.reshape(nodes, lat),
        edge_cot,
    )
    outs = pl.pallas_call(
        write_out,
        out_shape=out_shape,
        in_specs=[hbm] * 7,
        out_specs=[hbm] * 7,
        scratch_shapes=[pltpu.VMEM(out.shape, out.dtype) for out in out_shape]
        + [dma((7,)), dma((7,))],
        compiler_params=pltpu.CompilerParams(vmem_limit_bytes=vmem_limit),
        name="write_results",
    )(*outs)
    return (outs[0].reshape(node_feat.shape), *outs[1:])


def solution(mesh):
    in_specs = (
        P("dom", "sub", None),
        P(("dom", "sub"), None),
        P(("dom", "sub")),
        P(("dom", "sub")),
        P(("dom", "sub")),
        P("dom", None),
        P("dom", None),
        P("dom", None),
        P("dom", None),
        P(None, "dom"),
        P("dom", "sub", None),
        P(("dom", "sub"), None),
    )
    out_specs = (
        P("dom", "sub", None),
        P(("dom", "sub"), None),
        P("dom", None),
        P("dom", None),
        P("dom", None),
        P("dom", None),
        P(None, "dom"),
    )
    return jax.shard_map(shards, mesh=mesh, in_specs=in_specs, out_specs=out_specs, check_vma=False)
```
